32 devices in a mesh: dp: 8 (over z, x), mp: 4 (over y, core).
Axes of the slice: x: 2, y: 2, z: 4, core: 2. Of those that a mesh axis runs over, the one named last changes fastest.
Arguments:
- inputs: bfloat16 [4096, 2048], P('dp'), may hold values from -8 to 8
- seq_lengths: int32 [8], P('dp'), may hold values from 64 to 512, as said below
- norm_in: float32 [2048], replicated, may hold values from 0.25 to 1.75
- w_query: bfloat16 [2048, 2048], P(None, 'mp'), may hold values from -0.125 to 0.125
- w_key: bfloat16 [2048, 128], replicated, may hold values from -0.125 to 0.125
- w_value: bfloat16 [2048, 128], replicated, may hold values from -0.125 to 0.125
- w_out: bfloat16 [2048, 2048], P('mp'), may hold values from -0.5 to 0.5
- norm_mid: float32 [2048], replicated, may hold values from 0.25 to 1.75
- w_gate: bfloat16 [2048, 5632], P(None, 'mp'), may hold values from -0.125 to 0.125
- w_up: bfloat16 [2048, 5632], P(None, 'mp'), may hold values from -0.125 to 0.125
- w_down: bfloat16 [5632, 2048], P('mp'), may hold values from -0.078125 to 0.078125
- out_cotangent: bfloat16 [4096, 2048], P('dp'), may hold values from -8 to 8
- kv_cotangent: bfloat16 [4096, 256], P('dp'), may hold values from -6 to 6
Outputs:
- result: bfloat16 [4096, 2048], P('dp')
- grad_inputs: bfloat16 [4096, 2048], P('dp')
- grad_norm_in: float32 [2048], P('dp')
- grad_w_query: float32 [2048, 2048], P('dp', 'mp')
- grad_w_key: float32 [2048, 128], P('dp')
- grad_w_value: float32 [2048, 128], P('dp')
- grad_w_out: float32 [2048, 2048], P('mp', 'dp')
- grad_norm_mid: float32 [2048], P('dp')
- grad_w_gate: float32 [2048, 5632], P('dp', 'mp')
- grad_w_up: float32 [2048, 5632], P('dp', 'mp')
- grad_w_down: float32 [5632, 2048], P('mp', 'dp')
The draws below stay inside these ranges and needn't reach their ends.
Inputs may be any that keep to these rules, and one draw needn't show every extreme that they name: Each dp index holds one sequence in the first seq_lengths of its 512 slots, the rest padding; one sequence has exactly 512 tokens and another exactly 64.
All inputs are finite; a program needn't handle non-finite values.
Results may differ from the reference program's by a relative error of at most 0.015.
Values sent between devices are 32-bit elements; how exact they have to be, the bound alone decides.
No kernel may reach another device: no remote copies, remote signals or barrier semaphores. Data moves between devices by JAX's collectives and lax.ppermute only.
A program may use at most 192 MiB of HBM per device.

```python
from functools import partial
import jax
import jax.numpy as jnp
from jax import lax

D = 2048
HEADS = 16
HEAD = 128
FF = 5632
SEQ_LEN = 512
MIN_LEN = 64
TOKENS = 4096
N_DP = 8


def draw_seq_lengths(key, part):
    key = jax.random.fold_in(key, 7)
    key_one, key_two, key_three = jax.random.split(key, 3)
    drawn = jax.random.randint(key_one, (N_DP,), MIN_LEN, SEQ_LEN + 1)
    longest = jax.random.randint(key_two, (), 0, N_DP)
    shortest = (longest + 1 + jax.random.randint(key_three, (), 0, N_DP - 1)) % N_DP
    drawn = drawn.at[shortest].set(MIN_LEN).at[longest].set(SEQ_LEN)
    return drawn.astype(jnp.int32)


def strengthened(values, rng, source, target, blocks, factor):
    owner, partner = [(jnp.arange(values.shape[dim]) // (values.shape[dim] // blocks)).reshape([-1 if axis == dim else 1 for axis in range(values.ndim)]) for dim in (source, target)]
    chosen = jax.random.permutation(rng, blocks)[partner]
    strong = (owner == chosen) | (owner == (partner + blocks // 2) % blocks)
    return jnp.where(strong, factor * values, values)


def level_of(own_key, extent, pieces, least, largest):
    def one(axis_at, blocks):
        draws = jax.random.uniform(jax.random.fold_in(jax.random.fold_in(own_key, 6), axis_at), (blocks,), jnp.float32, least / len(pieces), largest / len(pieces))
        return jnp.repeat(jnp.exp(draws), extent[axis_at] // blocks).reshape((-1,) + (1,) * (len(extent) - axis_at - 1))

    loudness = one(*pieces[0])
    for cut in pieces[1:]:
        loudness = loudness * one(*cut)
    return loudness


def scatter_about(rng, shape, width, reach, pieces=(), kind=jnp.bfloat16):
    loudness = level_of(rng, shape, pieces, -0.22, 0.18) if pieces else 1.0
    array = jax.random.normal(rng, shape, jnp.float32) * width * loudness
    return jnp.minimum(jnp.maximum(array, -reach), reach).astype(kind)


def noise_with(rng, shape, spread, bound, pieces, heavy, held_as=jnp.bfloat16):
    values = spread * jax.random.normal(rng, shape, jnp.float32)
    if pieces:
        values = values * level_of(rng, shape, pieces, -0.22, 0.18)
    return jnp.clip(strengthened(values, jax.random.fold_in(rng, 3), *heavy), -bound, bound).astype(held_as)


def setup_inputs(seed: int = 0) -> dict:
    seeds = jax.random.split(jax.random.key(seed), 14)
    return {
        "inputs": noise_with(seeds[0], (TOKENS, D), 1.0, 8.0, ((0, 8),), (0, 1, 8, 2.0)),
        "seq_lengths": draw_seq_lengths(jax.random.fold_in(seeds[13], 71), 0),
        "norm_in": jnp.clip(1.0 + 0.15 * jax.random.normal(seeds[2], (D,), jnp.float32), 0.25, 1.75),
        "w_query": scatter_about(seeds[3], (D, HEADS * HEAD), D ** -0.5, 0.125, ((1, 4),)),
        "w_key": scatter_about(seeds[4], (D, HEAD), D ** -0.5, 0.125),
        "w_value": scatter_about(seeds[5], (D, HEAD), D ** -0.5, 0.125),
        "w_out": scatter_about(seeds[6], (HEADS * HEAD, D), (HEADS * HEAD // 16) ** -0.5, 0.5, ((0, 4),)),
        "norm_mid": jnp.clip(1.0 + 0.15 * jax.random.normal(seeds[7], (D,), jnp.float32), 0.25, 1.75),
        "w_gate": scatter_about(seeds[8], (D, FF), D ** -0.5, 0.125, ((1, 4),)),
        "w_up": scatter_about(seeds[9], (D, FF), D ** -0.5, 0.125, ((1, 4),)),
        "w_down": scatter_about(seeds[10], (FF, D), FF ** -0.5, 0.078125, ((0, 4),)),
        "out_cotangent": noise_with(seeds[11], (TOKENS, D), 1.0, 8.0, ((0, 8),), (0, 1, 8, 2.0)),
        "kv_cotangent": scatter_about(seeds[12], (TOKENS, 2 * HEAD), 1.0, 6.0, ((0, 8),)),
    }


epsilon = 1e-06
highest = lax.Precision.HIGHEST
masked_value = -1e+30

@jax.custom_vjp
def low(v):
    return lax.optimization_barrier(v.astype(jnp.bfloat16)).astype(jnp.float32)

@jax.custom_vjp
def low_back(v):
    return v

def low_keep(v):
    return (low(v), None)

def low_pass(kept, grad):
    return (grad,)

def back_keep(v):
    return (v, None)

def back_low(kept, grad):
    return (low(grad),)
low.defvjp(low_keep, low_pass)
low_back.defvjp(back_keep, back_low)

def rotary_tables(length, size):
    half_size = size // 2
    inverse = 10000.0 ** (-2.0 * jnp.arange(half_size, dtype=jnp.float32) / size)
    angles = jnp.arange(length, dtype=jnp.float32)[:, None] * inverse[None, :]
    return (jnp.cos(angles), jnp.sin(angles))

def rotate(values, cosine_table, sine_table):
    half_size = values.shape[-1] // 2
    front_half = values[..., :half_size]
    back_half = values[..., half_size:]
    return jnp.concatenate([front_half * cosine_table - back_half * sine_table, back_half * cosine_table + front_half * sine_table], axis=-1)

def rms_scale(stream, gain):
    return stream * lax.rsqrt(lax.optimization_barrier(jnp.mean(stream * stream, axis=-1, keepdims=True)) + epsilon) * gain

def matmul(left, right):
    return jnp.dot(left, right, precision=highest)

def one_sequence(packed):
    queries, key_rot, value_rows, length = packed
    position = jnp.arange(SEQ_LEN)
    scores = low_back(jnp.einsum('hqe,ke->hqk', queries, key_rot, precision=highest) * HEAD ** (-0.5))
    allowed = (position[None, :] <= position[:, None]) & (position[None, :] < length)
    scores = jnp.where(allowed[None], scores, masked_value)
    row_max = lax.optimization_barrier(jnp.max(scores, axis=-1, keepdims=True))
    exponent = jnp.exp(scores - row_max)
    weights = low(exponent / lax.optimization_barrier(jnp.sum(exponent, axis=-1, keepdims=True)))
    valid_rows = (position < length).astype(jnp.float32)
    return jnp.einsum('hqk,ke->hqe', weights, value_rows, precision=highest) * valid_rows[None, :, None]

def layer(stream, norm_in, w_query, w_key, w_value, w_out, norm_mid, w_gate, w_up, w_down, seq_lengths):
    cosine_table, sine_table = rotary_tables(SEQ_LEN, HEAD)
    normed = low(rms_scale(stream, norm_in))
    queries = low_back(matmul(normed, w_query)).reshape(N_DP, SEQ_LEN, HEADS, HEAD)
    queries = low(rotate(queries, cosine_table[None, :, None, :], sine_table[None, :, None, :]))
    key_raw = low_back(matmul(normed, w_key)).reshape(N_DP, SEQ_LEN, HEAD)
    key_rot = low(rotate(key_raw, cosine_table[None], sine_table[None]))
    value_rows = low(low_back(matmul(normed, w_value))).reshape(N_DP, SEQ_LEN, HEAD)
    attended = lax.map(jax.checkpoint(one_sequence), (queries.transpose(0, 2, 1, 3), key_rot, value_rows, seq_lengths))
    attended = low(low_back(attended.transpose(0, 2, 1, 3).reshape(N_DP * SEQ_LEN, HEADS * HEAD)))
    hidden_stream = stream + low_back(matmul(attended, w_out))
    normed_mid = low(rms_scale(hidden_stream, norm_mid))
    gate_value = low_back(matmul(normed_mid, w_gate))
    up_value = low_back(matmul(normed_mid, w_up))
    mixed = low(low_back(gate_value * jax.nn.sigmoid(gate_value) * up_value))
    result = hidden_stream + low_back(matmul(mixed, w_down))
    shared = jnp.concatenate([key_rot.reshape(N_DP * SEQ_LEN, HEAD), value_rows.reshape(N_DP * SEQ_LEN, HEAD)], axis=-1)
    return (result, shared)

def reference(inputs, seq_lengths, norm_in, w_query, w_key, w_value, w_out, norm_mid, w_gate, w_up, w_down, out_cotangent, kv_cotangent):
    position = jnp.arange(N_DP * SEQ_LEN) % SEQ_LEN
    bounds = jnp.repeat(seq_lengths, SEQ_LEN, total_repeat_length=N_DP * SEQ_LEN)
    valid_rows = (position < bounds).astype(jnp.float32)[:, None]
    forward = partial(layer, seq_lengths=seq_lengths)
    (result, shared), pullback = jax.vjp(forward, inputs.astype(jnp.float32), norm_in.astype(jnp.float32), w_query.astype(jnp.float32), w_key.astype(jnp.float32), w_value.astype(jnp.float32), w_out.astype(jnp.float32), norm_mid.astype(jnp.float32), w_gate.astype(jnp.float32), w_up.astype(jnp.float32), w_down.astype(jnp.float32))
    grads = pullback((out_cotangent.astype(jnp.float32) * valid_rows, kv_cotangent.astype(jnp.float32) * valid_rows))
    return (result.astype(jnp.bfloat16), grads[0].astype(jnp.bfloat16), grads[1], grads[2], grads[3], grads[4], grads[5], grads[6], grads[7], grads[8], grads[9])
```

```python
import jax
import jax.numpy as jnp
from jax import lax
from jax.sharding import Mesh, PartitionSpec as P

epsilon = 1e-06
masked_value = -1e30
GROUP = 4
f32 = jnp.float32
bf16 = jnp.bfloat16


def dot(a, b):
    return jnp.dot(a, b, preferred_element_type=f32)


def dot_nt(a, b):
    return lax.dot_general(a, b, (((1,), (1,)), ((), ())), preferred_element_type=f32)


def dot_tn(a, b):
    return lax.dot_general(a, b, (((0,), (0,)), ((), ())), preferred_element_type=f32)


def swap(a, axis):
    return lax.ppermute(a, axis, [(0, 1), (1, 0)])


def relative(a):
    q = a.shape[0] // 4
    c, y = lax.axis_index("c"), lax.axis_index("y")
    me = 2 * c + y
    parts = [lax.dynamic_slice_in_dim(a, (me ^ k) * q, q, 0) for k in range(4)]
    return jnp.concatenate(parts, axis=0)


def rotary_tables(positions, size):
    half_size = size // 2
    inverse = 10000.0 ** (-2.0 * jnp.arange(half_size, dtype=f32) / size)
    angles = positions.astype(f32)[:, None] * inverse[None, :]
    return (jnp.cos(angles), jnp.sin(angles))


def rotate(values, cosine_table, sine_table):
    half_size = values.shape[-1] // 2
    a, b = values[..., :half_size], values[..., half_size:]
    return jnp.concatenate([a * cosine_table - b * sine_table, b * cosine_table + a * sine_table], axis=-1)


def unrotate(values, cosine_table, sine_table):
    return rotate(values, cosine_table, -sine_table)


def norm_back(stream, inverse_rms, gain, grad_normed):
    weighted = gain * grad_normed
    return inverse_rms * weighted - stream * inverse_rms**3 * jnp.mean(weighted * stream, axis=-1, keepdims=True)


def reduce_half(part):
    h = part.shape[0] // 2
    q = h // 2
    mine = part[:h] + swap(part[h:], "c")
    own = mine[:q] + swap(mine[q:], "y")
    return jnp.concatenate([own, swap(own, "y")], axis=0)


def reduce_full(part):
    half = reduce_half(part)
    return jnp.concatenate([half, swap(half, "c")], axis=0)


def remote_blocks(gathered):
    z = lax.axis_index("z")
    return jnp.stack(
        [
            lax.dynamic_index_in_dim(gathered, lax.rem(z + k, GROUP), 0, keepdims=False)
            for k in range(1, GROUP)
        ]
    )


def ffn_pre(normed_mid, w_gate, w_up):
    gate = dot(normed_mid, w_gate)
    up = dot(normed_mid, w_up)
    sig = jax.nn.sigmoid(gate)
    return gate, up, sig


def ffn_back(gate, up, sig, grad_mixed):
    grad_mixed = grad_mixed.astype(bf16).astype(f32)
    grad_gate = (grad_mixed * up * sig * (1.0 + gate * (1.0 - sig))).astype(bf16)
    grad_up = (grad_mixed * gate * sig).astype(bf16)
    return grad_gate, grad_up


def scores_of(query_block, key_rot, pos_q, pos_k, length, score_scale):
    scores = jnp.einsum("qhe,ke->hqk", query_block, key_rot, preferred_element_type=f32) * score_scale
    allowed = (pos_k[None, :] <= pos_q[:, None]) & (pos_k[None, :] < length)
    return jnp.where(allowed[None], scores, masked_value)


def shards(
    sizes,
    inputs,
    seq_lengths,
    norm_in,
    w_query,
    w_key,
    w_value,
    w_out,
    norm_mid,
    w_gate,
    w_up,
    w_down,
    out_cotangent,
    kv_cotangent,
):
    n_outer, n_dp = sizes
    dp_axes = ("o", "z", "x")
    seq_len, width = inputs.shape
    half, quarter = seq_len // 2, seq_len // 4
    head = w_key.shape[1]
    heads = w_query.shape[1] // head
    score_scale = head ** (-0.5)
    rows = width // n_dp
    z, x = lax.axis_index("z"), lax.axis_index("x")
    length = seq_lengths[0]
    one = jnp.minimum(length, 1).astype(f32)
    positions = relative(jnp.arange(seq_len))
    valid = (positions < length).astype(f32)[:, None]
    stream = relative(inputs).astype(f32)
    grad_out = relative(out_cotangent).astype(f32) * valid
    cosine, sine = rotary_tables(positions, head)

    go_z = lax.all_gather(grad_out[:quarter], "z", axis=0, tiled=False)

    inverse_in = lax.rsqrt(jnp.mean(stream * stream, axis=-1, keepdims=True) + epsilon)
    normed = (stream * inverse_in * norm_in).astype(bf16)
    queries = dot(normed, w_query).reshape(seq_len, heads, head)
    queries = rotate(queries, cosine[:, None, :], sine[:, None, :]).astype(bf16)
    key_rot = rotate(dot(normed, w_key), cosine, sine).astype(bf16)
    value_rows = dot(normed, w_value).astype(bf16)
    attended, logs = [], []
    for b in range(2):
        at = slice(b * half, (b + 1) * half)
        scores = scores_of(queries[at], key_rot, positions[at], positions, length, score_scale)
        row_max = jnp.max(scores, axis=-1, keepdims=True)
        exponent = jnp.exp(scores - row_max)
        totals = jnp.sum(exponent, axis=-1, keepdims=True)
        weights = (exponent / totals).astype(bf16)
        out = jnp.einsum("hqk,ke->qhe", weights, value_rows, preferred_element_type=f32)
        attended.append((out * valid[at][:, :, None]).astype(bf16))
        logs.append(row_max + jnp.log(totals))
    attended = jnp.concatenate(attended, axis=0).reshape(seq_len, heads * head)
    hidden_half = stream[:half] + reduce_half(dot(attended, w_out))
    hidden = jnp.concatenate([hidden_half, swap(hidden_half, "c")], axis=0)

    scaled_half = hidden_half * lax.rsqrt(jnp.mean(hidden_half * hidden_half, axis=-1, keepdims=True) + epsilon)
    nm_z = lax.all_gather(scaled_half, "z", axis=0, tiled=False)

    inverse_mid = lax.rsqrt(jnp.mean(hidden * hidden, axis=-1, keepdims=True) + epsilon)
    normed_mid = (hidden * inverse_mid * norm_mid).astype(bf16)
    gate, up, sig = ffn_pre(normed_mid, w_gate, w_up)
    mixed = (gate * sig * up).astype(bf16)
    grad_down_in = grad_out.astype(bf16)
    grad_gate, grad_up = ffn_back(gate, up, sig, dot_nt(grad_down_in, w_down))
    mid_part = dot_nt(grad_gate, w_gate) + dot_nt(grad_up, w_up)
    grad_normed_mid = reduce_full(mid_part)
    result = hidden + reduce_full(dot(mixed, w_down))
    grad_norm_mid = jnp.sum(grad_normed_mid * hidden * inverse_mid, axis=0)
    grad_hidden = grad_out + norm_back(hidden, inverse_mid, norm_mid, grad_normed_mid)

    grad_attention = grad_hidden.astype(bf16)
    grad_w_out = dot_tn(attended, grad_attention)
    grad_w_out = lax.psum_scatter(grad_w_out, dp_axes, scatter_dimension=1, tiled=True)
    grad_attended = (dot_nt(grad_attention, w_out).astype(bf16) * valid.astype(bf16)).reshape(seq_len, heads, head)
    grad_queries = []
    grad_key = jnp.zeros((seq_len, head), f32)
    grad_value = jnp.zeros((seq_len, head), f32)
    for b in range(2):
        at = slice(b * half, (b + 1) * half)
        scores = scores_of(queries[at], key_rot, positions[at], positions, length, score_scale)
        probs = jnp.exp(scores - logs[b])
        grad_probs = jnp.einsum("qhe,ke->hqk", grad_attended[at], value_rows, preferred_element_type=f32)
        delta = jnp.sum(probs * grad_probs, axis=-1, keepdims=True)
        grad_scores = (probs * (grad_probs - delta)).astype(bf16)
        grad_queries.append(jnp.einsum("hqk,ke->qhe", grad_scores, key_rot, preferred_element_type=f32) * score_scale)
        grad_key += jnp.einsum("hqk,qhe->ke", grad_scores, queries[at], preferred_element_type=f32) * score_scale
        grad_value += jnp.einsum("hqk,qhe->ke", probs.astype(bf16), grad_attended[at], preferred_element_type=f32)
    grad_query = unrotate(jnp.concatenate(grad_queries, axis=0), cosine[:, None, :], sine[:, None, :])
    grad_query = grad_query.astype(bf16).reshape(seq_len, heads * head)
    grad_w_query = dot_tn(normed, grad_query)
    grad_w_query = lax.psum_scatter(grad_w_query, dp_axes, scatter_dimension=0, tiled=True)
    grad_kv = reduce_full(jnp.concatenate([grad_key, grad_value], axis=1))
    summed_input = reduce_full(dot_nt(grad_query, w_query))
    grad_kv = grad_kv + relative(kv_cotangent).astype(f32) * valid
    grad_key = unrotate(grad_kv[:, :head], cosine, sine).astype(bf16)
    grad_value = grad_kv[:, head:].astype(bf16)
    grad_w_key = dot_tn(normed, grad_key)
    grad_w_value = dot_tn(normed, grad_value)
    grad_normed = summed_input + dot_nt(grad_key, w_key) + dot_nt(grad_value, w_value)
    grad_norm_in = jnp.sum(grad_normed * stream * inverse_in, axis=0)
    grad_inputs = grad_hidden + norm_back(stream, inverse_in, norm_in, grad_normed)

    piece = rows // 4
    m = 2 * lax.axis_index("y") + lax.axis_index("c")
    kv = jnp.concatenate([grad_w_key, grad_w_value], axis=1).reshape(n_dp, 4, piece, 2 * head)
    kv = lax.dynamic_index_in_dim(kv, m, 1, keepdims=False)
    gains = jnp.stack([grad_norm_in, grad_norm_mid]).reshape(2, n_dp, rows).transpose(1, 0, 2)
    gains = gains.reshape(n_dp, 2 * rows // (2 * head) if rows >= 2 * head else 2, -1)
    gains = jnp.pad(gains, ((0, 0), (0, 6), (0, 2 * head - gains.shape[2])))
    small = lax.psum_scatter(jnp.concatenate([kv, gains], axis=1), dp_axes, scatter_dimension=0, tiled=True)[0]
    kv = lax.all_gather(small[:piece], ("y", "c"), axis=0, tiled=True)
    out_norm_in, out_norm_mid = small[piece, :rows], small[piece + 1, :rows]

    go_own = remote_blocks(go_z)
    go_other = swap(go_own, "y")
    go_half = jnp.concatenate([go_own, go_other], axis=1)
    go_halves = (go_half, swap(go_half, "c"))
    nm_half = remote_blocks(nm_z)
    nm_halves = (nm_half, swap(nm_half, "c"))
    all_nm, all_go, all_mixed, all_gate, all_up = [normed_mid], [grad_down_in], [mixed], [grad_gate], [grad_up]
    for nm, go in zip(nm_halves, go_halves):
        nm = (nm.reshape(-1, width) * norm_mid).astype(bf16)
        go = (go.reshape(-1, width) * one).astype(bf16)
        gate, up, sig = ffn_pre(nm, w_gate, w_up)
        gg, gu = ffn_back(gate, up, sig, dot_nt(go, w_down))
        all_nm.append(nm)
        all_go.append(go)
        all_mixed.append((gate * sig * up).astype(bf16))
        all_gate.append(gg)
        all_up.append(gu)

    def columns(parts, which):
        taken = []
        for part in parts:
            part = part.reshape(-1, n_outer, GROUP, 2, rows)
            part = lax.dynamic_index_in_dim(part, z, 2, keepdims=False)
            part = lax.dynamic_index_in_dim(part, which, 2, keepdims=False)
            taken.append(part.reshape(-1, n_outer * rows))
        return jnp.concatenate(taken, axis=0)

    all_mixed = jnp.concatenate(all_mixed, axis=0)
    all_gate = jnp.concatenate(all_gate, axis=0)
    all_up = jnp.concatenate(all_up, axis=0)
    nm_send, nm_keep = columns(all_nm, 1 - x), columns(all_nm, x)
    go_send, go_keep = columns(all_go, 1 - x), columns(all_go, x)
    grad_w_down = dot_tn(all_mixed, go_keep) + swap(dot_tn(all_mixed, go_send), "x")
    grad_w_gate = dot_tn(nm_keep, all_gate) + swap(dot_tn(nm_send, all_gate), "x")
    grad_w_up = dot_tn(nm_keep, all_up) + swap(dot_tn(nm_send, all_up), "x")
    if n_outer > 1:
        grad_w_down = lax.psum_scatter(grad_w_down, "o", scatter_dimension=1, tiled=True)
        grad_w_gate = lax.psum_scatter(grad_w_gate, "o", scatter_dimension=0, tiled=True)
        grad_w_up = lax.psum_scatter(grad_w_up, "o", scatter_dimension=0, tiled=True)

    return (
        relative(result.astype(bf16)),
        relative(grad_inputs.astype(bf16)),
        out_norm_in,
        grad_w_query,
        kv[:, :head],
        kv[:, head:],
        grad_w_out,
        out_norm_mid,
        grad_w_gate,
        grad_w_up,
        grad_w_down,
    )


def solution(mesh):
    n_dp = mesh.shape["dp"]
    n_outer = n_dp // (2 * GROUP)
    split = Mesh(mesh.devices.reshape(n_outer, GROUP, 2, 2, 2), ("o", "z", "x", "y", "c"))
    dp, mp = ("o", "z", "x"), ("y", "c")

    def program(*args):
        return shards((n_outer, n_dp), *args)

    return jax.shard_map(
        program,
        mesh=split,
        in_specs=(
            P(dp, None),
            P(dp),
            P(),
            P(None, mp),
            P(),
            P(),
            P(mp, None),
            P(),
            P(None, mp),
            P(None, mp),
            P(mp, None),
            P(dp, None),
            P(dp, None),
        ),
        out_specs=(
            P(dp, None),
            P(dp, None),
            P(dp),
            P(dp, mp),
            P(dp, None),
            P(dp, None),
            P(mp, dp),
            P(dp),
            P(dp, mp),
            P(dp, mp),
            P(mp, dp),
        ),
        check_vma=False,
    )
```

```python
import functools

import jax
import jax.numpy as jnp
from jax import lax
from jax.experimental import pallas as pl
from jax.experimental.pallas import tpu as pltpu
from jax.sharding import Mesh, PartitionSpec as P

epsilon = 1e-06
masked_value = -1e30
GROUP = 4
f32 = jnp.float32
bf16 = jnp.bfloat16


def dot(a, b):
    return jnp.dot(a, b, preferred_element_type=f32)


def dot_nt(a, b):
    return lax.dot_general(a, b, (((1,), (1,)), ((), ())), preferred_element_type=f32)


def dot_tn(a, b):
    return lax.dot_general(a, b, (((0,), (0,)), ((), ())), preferred_element_type=f32)


def swap(a, axis):
    return lax.ppermute(a, axis, [(0, 1), (1, 0)])


def relative(a):
    q = a.shape[0] // 4
    c, y = lax.axis_index("c"), lax.axis_index("y")
    me = 2 * c + y
    parts = [lax.dynamic_slice_in_dim(a, (me ^ k) * q, q, 0) for k in range(4)]
    return jnp.concatenate(parts, axis=0)


def rotary_tables(positions, size):
    half_size = size // 2
    inverse = 10000.0 ** (-2.0 * jnp.arange(half_size, dtype=f32) / size)
    angles = positions.astype(f32)[:, None] * inverse[None, :]
    cosine, sine = jnp.cos(angles), jnp.sin(angles)
    return jnp.concatenate([cosine, cosine], axis=1), jnp.concatenate([-sine, sine], axis=1)


def rotate(values, same, crossed):
    return values * same + pltpu.roll(values, values.shape[-1] // 2, 1) * crossed


def norm_back(stream, inverse_rms, gain, grad_normed):
    weighted = gain * grad_normed
    return inverse_rms * weighted - stream * inverse_rms**3 * jnp.mean(weighted * stream, axis=-1, keepdims=True)


def inverse_rms(block):
    return lax.rsqrt(jnp.mean(block * block, axis=-1, keepdims=True) + epsilon)


class Link:
    def __init__(self, axis):
        self.axis = axis
        self.last = ()

    def move(self, a, pairs):
        a = lax.optimization_barrier((a, *self.last))[0]
        a = lax.ppermute(a, self.axis, pairs)
        self.last = (a,)
        return a

    def swap(self, a):
        return self.move(a, [(0, 1), (1, 0)])

    def pair(self, a, bit):
        return self.move(a, [(i, i ^ bit) for i in range(GROUP)])


def reduce_quarter(part, y_link):
    h = part.shape[0] // 2
    q = h // 2
    kept = part[:h] + swap(part[h:], "c")
    return kept[:q] + y_link.swap(kept[q:])


def spread(own, y_link):
    other = y_link.swap(own)
    return [own, other, swap(own, "c"), swap(other, "c")]


def halve(a, axis, mine, exchange):
    n = a.shape[axis] // 2
    kept = lax.dynamic_slice_in_dim(a, mine * n, n, axis)
    return kept + exchange(lax.dynamic_slice_in_dim(a, (1 - mine) * n, n, axis))


def scatter_z(a, axis, n_outer, z_link):
    if n_outer > 1:
        return lax.psum_scatter(a, ("o", "z"), scatter_dimension=axis, tiled=True)
    z = lax.axis_index("z")
    a = halve(a, axis, z // 2, lambda v: z_link.pair(v, 2))
    return halve(a, axis, z % 2, lambda v: z_link.pair(v, 1))


def by_x(a, which, rows):
    n = a.shape[1] // (2 * rows)
    return jnp.concatenate([lax.dynamic_slice_in_dim(a, (2 * i + which) * rows, rows, 1) for i in range(n)], axis=1)


def call(kernel, name, ins, outs, flops=0, transcendentals=0):
    moved = sum(a.size * a.dtype.itemsize for a in (*ins, *outs))
    return pl.pallas_call(
        kernel,
        out_shape=outs,
        name=name,
        compiler_params=pltpu.CompilerParams(vmem_limit_bytes=56 * 2**20),
        cost_estimate=pl.CostEstimate(flops=flops, bytes_accessed=moved, transcendentals=transcendentals),
    )(*ins)


def probabilities(q, k, allowed, scale):
    scores = jnp.where(allowed, dot_nt(q, k) * scale, masked_value)
    exponent = jnp.exp(scores - jnp.max(scores, axis=-1, keepdims=True))
    return exponent / jnp.sum(exponent, axis=-1, keepdims=True)


def forward_kernel(
    scale, x_ref, gain_ref, wq_ref, wk_ref, wv_ref, wo_ref, same_ref, crossed_ref, pos_q_ref, pos_k_ref, length_ref,
    part_ref, normed_ref, q_ref, k_ref, v_ref, attended_ref,
):
    stream = x_ref[...].astype(f32)
    normed_ref[...] = (stream * inverse_rms(stream) * gain_ref[...]).astype(bf16)
    normed = normed_ref[...]
    same, crossed = same_ref[...], crossed_ref[...]
    k = rotate(dot(normed, wk_ref[...]), same, crossed).astype(bf16)
    v = dot(normed, wv_ref[...]).astype(bf16)
    k_ref[...], v_ref[...] = k, v
    raw = dot(normed, wq_ref[...])
    length = length_ref[0, 0]
    allowed = (pos_k_ref[...] <= pos_q_ref[...]) & (pos_k_ref[...] < length)
    valid = (pos_q_ref[...] < length).astype(f32)
    size = k.shape[1]
    for h in range(raw.shape[1] // size):
        at = slice(h * size, (h + 1) * size)
        q = rotate(raw[:, at], same, crossed).astype(bf16)
        q_ref[:, at] = q
        weights = probabilities(q, k, allowed, scale).astype(bf16)
        attended_ref[:, at] = (dot(weights, v) * valid).astype(bf16)
    part_ref[...] = dot(attended_ref[...], wo_ref[...])


def backward_kernel(
    scale, ga_ref, wo_ref, wq_ref, q_ref, k_ref, v_ref, same_ref, crossed_ref, pos_q_ref, pos_k_ref, length_ref,
    part_ref, kv_ref, gq_ref,
):
    k, v = k_ref[...], v_ref[...]
    same, crossed = same_ref[...], crossed_ref[...]
    length = length_ref[0, 0]
    allowed = (pos_k_ref[...] <= pos_q_ref[...]) & (pos_k_ref[...] < length)
    valid = (pos_q_ref[...] < length).astype(f32)
    grad_attended = (dot_nt(ga_ref[...], wo_ref[...]) * valid).astype(bf16)
    size = k.shape[1]
    grad_key = grad_value = 0.0
    for h in range(grad_attended.shape[1] // size):
        at = slice(h * size, (h + 1) * size)
        q, g = q_ref[:, at], grad_attended[:, at]
        probs = probabilities(q, k, allowed, scale)
        grad_probs = dot_nt(g, v)
        delta = jnp.sum(probs * grad_probs, axis=-1, keepdims=True)
        grad_scores = (probs * (grad_probs - delta)).astype(bf16)
        gq_ref[:, at] = rotate(dot(grad_scores, k) * scale, same, -crossed).astype(bf16)
        grad_key += dot_tn(grad_scores, q)
        grad_value += dot_tn(probs.astype(bf16), g)
    kv_ref[:, :size] = grad_key * scale
    kv_ref[:, size:] = grad_value
    part_ref[...] = dot_nt(gq_ref[...], wq_ref[...])


def rows_call(kernel, name, quarters, stacked, shared, outs, totals, tile=16, prefetch=()):
    count, width = quarters[0][0].shape
    args = [a for group in quarters for a in group] + list(stacked) + list(shared)
    specs = [pl.BlockSpec((tile, width), lambda t, *p: (t, 0))] * (4 * len(quarters))
    specs += [pl.BlockSpec((4, tile, a.shape[2]), lambda t, *p: (0, t, 0)) for a in stacked]
    specs += [pl.BlockSpec(a.shape, lambda t, *p: (0, 0)) for a in shared]
    out_specs = [pl.BlockSpec((4, tile, w), lambda t, *p: (0, t, 0)) for w, _ in outs]
    out_specs += [pl.BlockSpec((1, width), lambda t, *p: (0, 0))] * totals
    out_shape = [jax.ShapeDtypeStruct((4, count, w), kind) for w, kind in outs]
    out_shape += [jax.ShapeDtypeStruct((1, width), f32)] * totals
    moved = sum(a.size * a.dtype.itemsize for a in (*args, *out_shape))
    return pl.pallas_call(
        kernel,
        grid_spec=pltpu.PrefetchScalarGridSpec(
            num_scalar_prefetch=len(prefetch), grid=(count // tile,), in_specs=specs, out_specs=out_specs
        ),
        out_shape=out_shape,
        name=name,
        compiler_params=pltpu.CompilerParams(vmem_limit_bytes=32 * 2**20),
        cost_estimate=pl.CostEstimate(flops=20 * count * width, bytes_accessed=moved, transcendentals=0),
    )(*prefetch, *args)


def mid_kernel(*refs):
    hidden, (gain, out) = refs[:4], refs[4:]
    for j in range(4):
        h = hidden[j][...]
        out[j] = (h * inverse_rms(h) * gain[...]).astype(bf16)


def mid_back_kernel(*refs):
    grads, hidden, (grad_out, gain, grad_hidden, rounded, total) = refs[:4], refs[4:8], refs[8:]
    gain = gain[...]
    acc = 0.0
    for j in range(4):
        h, g = hidden[j][...], grads[j][...]
        r = inverse_rms(h)
        acc += jnp.sum(g * h * r, axis=0, keepdims=True)
        back = grad_out[j].astype(f32) + norm_back(h, r, gain, g)
        grad_hidden[j] = back
        rounded[j] = back.astype(bf16)

    @pl.when(pl.program_id(0) == 0)
    def _():
        total[...] = jnp.zeros_like(total)

    total[...] += acc


def in_back_kernel(*refs):
    sums, (keyed, inputs, grad_hidden, gain, out, total) = refs[:4], refs[4:]
    gain = gain[...]
    acc = 0.0
    for j in range(4):
        stream = inputs[j].astype(f32)
        g = sums[j][...] + keyed[j]
        r = inverse_rms(stream)
        acc += jnp.sum(g * stream * r, axis=0, keepdims=True)
        out[j] = (grad_hidden[j] + norm_back(stream, r, gain, g)).astype(bf16)

    @pl.when(pl.program_id(0) == 0)
    def _():
        total[...] = jnp.zeros_like(total)

    total[...] += acc


def add_kernel(*refs):
    left, right, (out,) = refs[:4], refs[4:8], refs[8:]
    for j in range(4):
        out[j] = (left[j][...] + right[j][...]).astype(bf16)


def pack_kernel(n, places, *refs):
    blocks, scale, out, picked = refs[:n], refs[n], refs[n + 1], refs[n + 2]
    width = picked.shape[2] // 2
    for j in range(n):
        out[j] = (blocks[j][...] * scale[...]).astype(bf16)
        for part in range(2):
            at = pl.ds(pl.multiple_of(places[part] * width, width), width)
            picked[j, :, part * width : (part + 1) * width] = (blocks[j][:, at] * scale[:, at]).astype(bf16)


def pack(blocks, scale, places, rows, tile=32):
    n = len(blocks)
    count, width = blocks[0].shape
    block = pl.BlockSpec((tile, width), lambda t, places: (t, 0))
    out, picked = pl.pallas_call(
        functools.partial(pack_kernel, n),
        grid_spec=pltpu.PrefetchScalarGridSpec(
            num_scalar_prefetch=1,
            grid=(count // tile,),
            in_specs=[block] * n + [pl.BlockSpec((1, width), lambda t, places: (0, 0))],
            out_specs=[
                pl.BlockSpec((n, tile, width), lambda t, places: (0, t, 0)),
                pl.BlockSpec((n, tile, 2 * rows), lambda t, places: (0, t, 0)),
            ],
        ),
        out_shape=[
            jax.ShapeDtypeStruct((n, count, width), bf16),
            jax.ShapeDtypeStruct((n, count, 2 * rows), bf16),
        ],
        compiler_params=pltpu.CompilerParams(vmem_limit_bytes=32 * 2**20),
        cost_estimate=pl.CostEstimate(flops=n * count * width, bytes_accessed=6 * n * count * width, transcendentals=0),
    )(places, *blocks, scale.reshape(1, width))
    return out.reshape(n * count, width), picked.reshape(n * count, 2 * rows)


def after(value, *others):
    return lax.optimization_barrier((value, *others))[0]


def ffn_kernel(own, has_prev, *refs):
    nm_ref, go_ref, nmc_ref, goc_ref, wg_ref, wu_ref, wd_ref = refs[:7]
    previous = refs[7:13] if has_prev else None
    outs = refs[13:] if has_prev else refs[7:]
    gate = dot(nm_ref[...], wg_ref[...])
    up = dot(nm_ref[...], wu_ref[...])
    grad_mixed = dot_nt(go_ref[...], wd_ref[...]).astype(bf16).astype(f32)
    sig = jax.nn.sigmoid(gate)
    gate_sig = gate * sig
    mixed = (gate_sig * up).astype(bf16)
    grad_gate = (grad_mixed * up * sig * (1.0 + gate * (1.0 - sig))).astype(bf16)
    grad_up = (grad_mixed * gate_sig).astype(bf16)
    n = nmc_ref.shape[1] // 2
    by_gate = dot_tn(nmc_ref[...], grad_gate)
    by_up = dot_tn(nmc_ref[...], grad_up)
    by_down = dot_tn(mixed, goc_ref[...])
    sums = (by_gate[:n], by_gate[n:], by_up[:n], by_up[n:], by_down[:, :n], by_down[:, n:])
    for i in range(6):
        outs[i][...] = sums[i] + previous[i][...] if has_prev else sums[i]
    if own:
        outs[6][...] = mixed
        outs[7][...] = grad_gate
        outs[8][...] = grad_up


def ffn(nm, go, nm_columns, go_columns, w_gate, w_up, w_down, previous=(), own=False, tile=512):
    count, width = nm.shape
    hidden = w_gate.shape[1]
    n = nm_columns.shape[1] // 2

    def whole(shape):
        return pl.BlockSpec(shape, lambda t: (0, 0), pipeline_mode=pl.Buffered(1))

    across = pl.BlockSpec((n, tile), lambda t: (0, t))
    down = pl.BlockSpec((tile, n), lambda t: (t, 0))
    sums = [across] * 4 + [down] * 2
    out_specs = list(sums)
    out_shape = [jax.ShapeDtypeStruct((n, hidden), f32)] * 4 + [jax.ShapeDtypeStruct((hidden, n), f32)] * 2
    if own:
        out_specs += [pl.BlockSpec((count, tile), lambda t: (0, t))] * 3
        out_shape += [jax.ShapeDtypeStruct((count, hidden), bf16)] * 3
    columns = pl.BlockSpec((width, tile), lambda t: (0, t))
    in_specs = [whole(nm.shape), whole(go.shape), whole(nm_columns.shape), whole(go_columns.shape)]
    in_specs += [columns, columns, pl.BlockSpec((tile, width), lambda t: (t, 0))]
    in_specs += sums if previous else []
    return pl.pallas_call(
        functools.partial(ffn_kernel, own, bool(previous)),
        grid=(pl.cdiv(hidden, tile),),
        in_specs=in_specs,
        out_specs=out_specs,
        out_shape=out_shape,
        compiler_params=pltpu.CompilerParams(vmem_limit_bytes=56 * 2**20),
        cost_estimate=pl.CostEstimate(
            flops=2 * count * hidden * (3 * width + 6 * n),
            bytes_accessed=6 * width * hidden + 4 * count * width + (48 if previous else 24) * n * hidden,
            transcendentals=count * hidden,
        ),
    )(nm, go, nm_columns, go_columns, w_gate, w_up, w_down, *previous)


def shards(
    sizes,
    inputs,
    seq_lengths,
    norm_in,
    w_query,
    w_key,
    w_value,
    w_out,
    norm_mid,
    w_gate,
    w_up,
    w_down,
    out_cotangent,
    kv_cotangent,
):
    n_outer, n_dp = sizes
    seq_len, width = inputs.shape
    quarter = seq_len // 4
    head = w_key.shape[1]
    own_heads = w_query.shape[1]
    scale = head ** (-0.5)
    rows = width // n_dp
    z, x = lax.axis_index("z"), lax.axis_index("x")
    y_link, x_link, z_link = Link("y"), Link("x"), Link("z")
    length = seq_lengths[0]
    one = jnp.minimum(length, 1).astype(f32)
    positions = relative(jnp.arange(seq_len))
    valid = (positions < length)[:, None]
    grad_down_in = jnp.where(valid, relative(out_cotangent), 0)
    go_quarter, inputs = lax.optimization_barrier((grad_down_in[:quarter].astype(f32), inputs))

    go_z = lax.all_gather(go_quarter, "z", axis=0, tiled=False)
    inputs = relative(inputs)
    stream_own = inputs[:quarter].astype(f32)
    gain_in, gain_mid = norm_in.reshape(1, width), norm_mid.reshape(1, width)
    same, crossed = rotary_tables(positions, head)
    masks = (same, crossed, positions[:, None], positions[None, :], seq_lengths.reshape(1, 1))

    def shape(n, kind):
        return jax.ShapeDtypeStruct((seq_len, n), kind)

    part, normed, queries, key_rot, value_rows, attended = call(
        functools.partial(forward_kernel, scale),
        "attention_forward",
        (inputs, gain_in, w_query, w_key, w_value, w_out, *masks),
        [shape(width, f32), shape(width, bf16), shape(own_heads, bf16), shape(head, bf16), shape(head, bf16),
         shape(own_heads, bf16)],
        flops=2 * seq_len * (width * (2 * own_heads + 2 * head) + 2 * seq_len * own_heads),
        transcendentals=seq_len * seq_len * own_heads // head,
    )
    hidden_own = stream_own + reduce_quarter(part, y_link)

    def scaled(block):
        return block * inverse_rms(block)

    def remote(gathered):
        return [lax.dynamic_index_in_dim(gathered, lax.rem(z + k, GROUP), 0, keepdims=False) for k in range(1, GROUP)]

    nm_z_own = lax.all_gather(scaled(hidden_own), "z", axis=0, tiled=False)
    hidden = spread(hidden_own, y_link)
    hidden[1], go_z = lax.optimization_barrier((hidden[1], go_z))
    nm_z_other = lax.all_gather(scaled(hidden[1]), "z", axis=0, tiled=False)
    go_remote = remote(go_z)
    go_other = [y_link.swap(block) for block in go_remote[:2]]

    def columns(part):
        part = part.reshape(part.shape[0], n_outer, GROUP, 2, rows) if n_outer > 1 else part
        taken = []
        for which in (1 - x, x):
            if n_outer > 1:
                cut = lax.dynamic_index_in_dim(part, z, 2, keepdims=False)
                cut = lax.dynamic_index_in_dim(cut, which, 2, keepdims=False)
                taken.append(cut.reshape(part.shape[0], n_outer * rows))
            else:
                taken.append(lax.dynamic_slice_in_dim(part, (2 * z + which) * rows, rows, 1))
        return jnp.concatenate(taken, axis=1)

    (normed_mid,) = rows_call(mid_kernel, "mid_norm", [hidden], [], [gain_mid], [(width, bf16)], 0)
    normed_mid = normed_mid.reshape(seq_len, width)
    weights = (w_gate, w_up, w_down)
    *sums, mixed, grad_gate, grad_up = ffn(
        normed_mid, grad_down_in, columns(normed_mid), columns(grad_down_in), *weights, own=True
    )
    mid_part = dot_nt(grad_gate, w_gate) + dot_nt(grad_up, w_up)
    mid_part, nm_z_own, *go_other = lax.optimization_barrier((mid_part, nm_z_own, *go_other))
    grad_mid = spread(reduce_quarter(mid_part, y_link), y_link)
    grad_hidden, grad_attention, grad_norm_mid = rows_call(
        mid_back_kernel, "mid_back", [grad_mid, hidden], [grad_down_in.reshape(4, quarter, width)], [gain_mid],
        [(width, f32), (width, bf16)], 1,
    )
    grad_attention = grad_attention.reshape(seq_len, width)

    go_other.append(y_link.swap(go_remote[2]))
    input_part, grad_kv, grad_query = call(
        functools.partial(backward_kernel, scale),
        "attention_backward",
        (grad_attention, w_out, w_query, queries, key_rot, value_rows, *masks),
        [shape(width, f32), shape(2 * head, f32), shape(own_heads, bf16)],
        flops=2 * seq_len * (2 * width * own_heads + 5 * seq_len * own_heads),
        transcendentals=seq_len * seq_len * own_heads // head,
    )
    input_part, go_other[2] = lax.optimization_barrier((input_part, go_other[2]))
    out_sent = x_link.swap(dot_tn(attended, by_x(grad_attention, 1 - x, rows)))
    out_kept = dot_tn(attended, by_x(grad_attention, x, rows))
    query_sent = x_link.swap(dot_tn(by_x(normed, 1 - x, rows), grad_query))
    query_kept = dot_tn(by_x(normed, x, rows), grad_query)
    grad_kv = jnp.concatenate(spread(reduce_quarter(grad_kv, y_link), y_link), axis=0)
    summed_own = reduce_quarter(input_part, y_link)
    summed_own, nm_z_other, out_sent = lax.optimization_barrier((summed_own, nm_z_other, out_sent))
    summed = spread(summed_own, y_link)
    grad_kv = grad_kv + jnp.where(valid, relative(kv_cotangent).astype(f32), 0.0)
    grad_key = grad_kv[:, :head]
    crossed_key = jnp.concatenate([grad_key[:, head // 2 :], grad_key[:, : head // 2]], axis=1)
    grad_key = (grad_key * same - crossed_key * crossed).astype(bf16)
    grad_value = grad_kv[:, head:].astype(bf16)
    grad_w_key = dot_tn(normed, grad_key)
    grad_w_value = dot_tn(normed, grad_value)
    keyed = dot_nt(grad_key, w_key) + dot_nt(grad_value, w_value)
    grad_inputs, grad_norm_in = rows_call(
        in_back_kernel, "in_back", [summed],
        [keyed.reshape(4, quarter, width), inputs.reshape(4, quarter, width), grad_hidden], [gain_in], [(width, bf16)], 1,
    )

    places = jnp.stack([2 * z + 1 - x, 2 * z + x]).astype(jnp.int32)
    nm_z_own = after(nm_z_own, grad_query)
    for nm, go in ((remote(nm_z_own), go_remote), (remote(nm_z_other), go_other)):
        nm = nm + [swap(block, "c") for block in nm]
        go = go + [swap(block, "c") for block in go]
        if n_outer == 1:
            nm, nm_columns = pack(nm, norm_mid, places, rows)
            go, go_columns = pack(go, jnp.ones_like(norm_mid), places, rows)
        else:
            nm = (jnp.concatenate(nm, axis=0) * norm_mid).astype(bf16)
            go = (jnp.concatenate(go, axis=0) * one).astype(bf16)
            nm_columns, go_columns = columns(nm), columns(go)
        sums = ffn(nm, go, nm_columns, go_columns, *weights, previous=sums)
    sums, query_sent = lax.optimization_barrier((sums, query_sent))
    grad_w_out = scatter_z(out_kept + out_sent, 1, n_outer, z_link)
    grad_w_query = scatter_z(query_kept + query_sent, 0, n_outer, z_link)
    grad_w_gate = sums[1] + x_link.swap(sums[0])
    grad_w_up = sums[3] + x_link.swap(sums[2])

    piece = rows // 4
    m = 2 * lax.axis_index("y") + lax.axis_index("c")
    kv = jnp.concatenate([grad_w_key, grad_w_value], axis=1).reshape(n_dp, 4, piece, 2 * head)
    kv = lax.dynamic_index_in_dim(kv, m, 1, keepdims=False)
    gains = jnp.concatenate([grad_norm_in, grad_norm_mid]).reshape(2, n_dp, rows).transpose(1, 0, 2)
    gains = jnp.pad(gains, ((0, 0), (0, 6), (0, 2 * head - rows)))
    small = jnp.concatenate([kv, gains], axis=1).reshape(n_dp // 2, 2, -1, 2 * head)
    small = halve(small, 1, x, x_link.swap)
    small = scatter_z(small.reshape(n_dp // 2, -1, 2 * head), 0, n_outer, z_link)[0]
    kv = lax.all_gather(small[:piece], ("y", "c"), axis=0, tiled=True)
    out_norm_in, out_norm_mid = small[piece, :rows], small[piece + 1, :rows]
    grad_w_down = sums[5] + x_link.swap(sums[4])

    down = spread(reduce_quarter(dot(after(mixed, summed[1]), w_down), y_link), y_link)
    (result,) = rows_call(add_kernel, "result", [down, hidden], [], [], [(width, bf16)], 0)
    if n_outer > 1:
        grad_w_down = lax.psum_scatter(grad_w_down, "o", scatter_dimension=1, tiled=True)
        grad_w_gate = lax.psum_scatter(grad_w_gate, "o", scatter_dimension=0, tiled=True)
        grad_w_up = lax.psum_scatter(grad_w_up, "o", scatter_dimension=0, tiled=True)

    return (
        relative(result.reshape(seq_len, width)),
        relative(grad_inputs.reshape(seq_len, width)),
        out_norm_in,
        grad_w_query,
        kv[:, :head],
        kv[:, head:],
        grad_w_out,
        out_norm_mid,
        grad_w_gate,
        grad_w_up,
        grad_w_down,
    )


def solution(mesh):
    n_dp = mesh.shape["dp"]
    n_outer = n_dp // (2 * GROUP)
    split = Mesh(mesh.devices.reshape(n_outer, GROUP, 2, 2, 2), ("o", "z", "x", "y", "c"))
    dp, mp = ("o", "z", "x"), ("y", "c")

    def program(*args):
        return shards((n_outer, n_dp), *args)

    return jax.shard_map(
        program,
        mesh=split,
        in_specs=(
            P(dp, None),
            P(dp),
            P(),
            P(None, mp),
            P(),
            P(),
            P(mp, None),
            P(),
            P(None, mp),
            P(None, mp),
            P(mp, None),
            P(dp, None),
            P(dp, None),
        ),
        out_specs=(
            P(dp, None),
            P(dp, None),
            P(dp),
            P(dp, mp),
            P(dp, None),
            P(dp, None),
            P(mp, dp),
            P(dp),
            P(dp, mp),
            P(dp, mp),
            P(mp, dp),
        ),
        check_vma=False,
    )
```

```python
import functools

import jax
import jax.numpy as jnp
from jax import lax
from jax.experimental import pallas as pl
from jax.experimental.pallas import tpu as pltpu
from jax.sharding import Mesh, PartitionSpec as P

epsilon = 1e-06
masked_value = -1e30
GROUP = 4
f32 = jnp.float32
bf16 = jnp.bfloat16

light = pl.CostEstimate(flops=1, bytes_accessed=1, transcendentals=0)


def dot(a, b):
    return jnp.dot(a, b, preferred_element_type=f32)


def dot_nt(a, b):
    return lax.dot_general(a, b, (((1,), (1,)), ((), ())), preferred_element_type=f32)


def dot_tn(a, b):
    return lax.dot_general(a, b, (((0,), (0,)), ((), ())), preferred_element_type=f32)


def arrange_kernel(places, length_ref, inputs_ref, cotangent_ref, kv_ref, inputs_out, cotangent_out, kv_out, quarter_out):
    k = pl.program_id(0)
    count = inputs_ref.shape[0]
    row = lax.broadcasted_iota(jnp.int32, (count, 1), 0) + places[k] * count
    valid = row < length_ref[0, 0]
    inputs_out[...] = inputs_ref[...]
    cotangent = jnp.where(valid, cotangent_ref[...].astype(f32), 0.0)
    cotangent_out[...] = cotangent.astype(bf16)
    kv_out[...] = jnp.where(valid, kv_ref[...].astype(f32), 0.0)

    @pl.when(k == 0)
    def _():
        quarter_out[...] = cotangent


def arrange(places, lengths, inputs, cotangent, kv):
    seq_len, width = inputs.shape
    q = seq_len // 4
    kv_width = kv.shape[1]
    picked = pl.BlockSpec((q, width), lambda k, p: (p[k], 0))
    placed = pl.BlockSpec((q, width), lambda k, p: (k, 0))
    return pl.pallas_call(
        arrange_kernel,
        grid_spec=pltpu.PrefetchScalarGridSpec(
            num_scalar_prefetch=1,
            grid=(4,),
            in_specs=[
                pl.BlockSpec((1, 1), lambda k, p: (0, 0)),
                picked,
                picked,
                pl.BlockSpec((q, kv_width), lambda k, p: (p[k], 0)),
            ],
            out_specs=[
                placed,
                placed,
                pl.BlockSpec((q, kv_width), lambda k, p: (k, 0)),
                pl.BlockSpec((q, width), lambda k, p: (0, 0)),
            ],
        ),
        out_shape=[
            jax.ShapeDtypeStruct((seq_len, width), bf16),
            jax.ShapeDtypeStruct((seq_len, width), bf16),
            jax.ShapeDtypeStruct((seq_len, kv_width), f32),
            jax.ShapeDtypeStruct((q, width), f32),
        ],
        name="arrange",
        compiler_params=pltpu.CompilerParams(vmem_limit_bytes=32 * 2**20),
        cost_estimate=light,
    )(places, lengths.reshape(1, 1), inputs, cotangent, kv)


def rotary_tables(positions, size):
    half_size = size // 2
    inverse = 10000.0 ** (-2.0 * jnp.arange(half_size, dtype=f32) / size)
    angles = positions.astype(f32)[:, None] * inverse[None, :]
    cosine, sine = jnp.cos(angles), jnp.sin(angles)
    return jnp.concatenate([cosine, cosine], axis=1), jnp.concatenate([-sine, sine], axis=1)


def rotate(values, same, crossed):
    return values * same + pltpu.roll(values, values.shape[-1] // 2, 1) * crossed


def norm_back(stream, inverse_rms, gain, grad_normed):
    weighted = gain * grad_normed
    return inverse_rms * weighted - stream * inverse_rms**3 * jnp.mean(weighted * stream, axis=-1, keepdims=True)


def inverse_rms(block):
    return lax.rsqrt(jnp.mean(block * block, axis=-1, keepdims=True) + epsilon)


def pack_z_kernel(places, *refs):
    blocks, (scale, out, picked) = refs[:6], refs[6:]
    width = picked.shape[2] // 2
    for j in range(6):
        out[j] = (blocks[j][0] * scale[...]).astype(bf16)
        for part in range(2):
            at = pl.ds(pl.multiple_of(places[part] * width, width), width)
            picked[j, :, part * width : (part + 1) * width] = (blocks[j][0, :, at] * scale[:, at]).astype(bf16)


def pack_z(own, far, scale, places, rows, tile=32):
    _, count, width = own.shape
    specs = [pl.BlockSpec((1, tile, width), lambda t, p, k=k: (p[2 + k], t, 0)) for k in range(GROUP - 1)]
    n = 2 * (GROUP - 1)
    out, picked = pl.pallas_call(
        pack_z_kernel,
        grid_spec=pltpu.PrefetchScalarGridSpec(
            num_scalar_prefetch=1,
            grid=(count // tile,),
            in_specs=specs + specs + [pl.BlockSpec((1, width), lambda t, p: (0, 0))],
            out_specs=[
                pl.BlockSpec((n, tile, width), lambda t, p: (0, t, 0)),
                pl.BlockSpec((n, tile, 2 * rows), lambda t, p: (0, t, 0)),
            ],
        ),
        out_shape=[
            jax.ShapeDtypeStruct((n, count, width), bf16),
            jax.ShapeDtypeStruct((n, count, 2 * rows), bf16),
        ],
        name="pack_z",
        compiler_params=pltpu.CompilerParams(vmem_limit_bytes=32 * 2**20),
        cost_estimate=light,
    )(places, *[own] * (GROUP - 1), *[far] * (GROUP - 1), scale.reshape(1, width))
    return out.reshape(n * count, width), picked.reshape(n * count, 2 * rows)


class Order:
    def __init__(self):
        self.core = ()
        self.links = {}

    def run(self, f, *args):
        n = len(args)
        args = lax.optimization_barrier((*args, *self.core))[:n]
        outs = f(*args)
        self.core = tuple(outs)[:1] if isinstance(outs, (list, tuple)) else (outs,)
        return outs

    def wait(self, a):
        (a,) = self.run(lambda a: lax.optimization_barrier((a,)), a)
        return a

    def move(self, a, axis, pairs, queue=True):
        before = self.links.get(axis, ()) if queue else ()
        a = lax.optimization_barrier((a, *self.core, *before))[0]
        a = lax.ppermute(a, axis, pairs)
        if queue:
            self.links[axis] = (a,)
        return a

    def swap(self, a, axis):
        return self.move(a, axis, [(0, 1), (1, 0)], queue=axis != "c")

    def pair_z(self, a, bit):
        return self.move(a, "z", [(i, i ^ bit) for i in range(GROUP)])


def split(a, axis, mine):
    n = a.shape[axis] // 2
    return lax.dynamic_slice_in_dim(a, mine * n, n, axis), lax.dynamic_slice_in_dim(a, (1 - mine) * n, n, axis)


def by_x(a, which, rows):
    n = a.shape[1] // (2 * rows)
    return jnp.concatenate([lax.dynamic_slice_in_dim(a, (2 * i + which) * rows, rows, 1) for i in range(n)], axis=1)


def call(kernel, name, ins, outs):
    return pl.pallas_call(
        kernel,
        out_shape=outs,
        name=name,
        compiler_params=pltpu.CompilerParams(vmem_limit_bytes=56 * 2**20),
        cost_estimate=light,
    )(*ins)


def probabilities(q, k, allowed, scale):
    scores = jnp.where(allowed, dot_nt(q, k) * scale, masked_value)
    exponent = jnp.exp(scores - jnp.max(scores, axis=-1, keepdims=True))
    return exponent / jnp.sum(exponent, axis=-1, keepdims=True)


def forward_kernel(
    scale, x_ref, gain_ref, wq_ref, wk_ref, wv_ref, wo_ref, same_ref, crossed_ref, pos_q_ref, pos_k_ref, length_ref,
    kept_ref, sent_ref, normed_ref, q_ref, k_ref, v_ref, attended_ref,
):
    stream = x_ref[...].astype(f32)
    normed_ref[...] = (stream * inverse_rms(stream) * gain_ref[...]).astype(bf16)
    normed = normed_ref[...]
    same, crossed = same_ref[...], crossed_ref[...]
    k = rotate(dot(normed, wk_ref[...]), same, crossed).astype(bf16)
    v = dot(normed, wv_ref[...]).astype(bf16)
    k_ref[...], v_ref[...] = k, v
    raw = dot(normed, wq_ref[...])
    length = length_ref[0, 0]
    allowed = (pos_k_ref[...] <= pos_q_ref[...]) & (pos_k_ref[...] < length)
    valid = (pos_q_ref[...] < length).astype(f32)
    size = k.shape[1]
    for h in range(raw.shape[1] // size):
        at = slice(h * size, (h + 1) * size)
        q = rotate(raw[:, at], same, crossed).astype(bf16)
        q_ref[:, at] = q
        weights = probabilities(q, k, allowed, scale).astype(bf16)
        attended_ref[:, at] = (dot(weights, v) * valid).astype(bf16)
    n = kept_ref.shape[0]
    sent_ref[...] = dot(attended_ref[n:], wo_ref[...])
    kept_ref[...] = dot(attended_ref[:n], wo_ref[...])


def backward_kernel(
    scale, ga_ref, wo_ref, wq_ref, q_ref, k_ref, v_ref, same_ref, crossed_ref, pos_q_ref, pos_k_ref, length_ref,
    kept_ref, sent_ref, kv_kept_ref, kv_sent_ref, gq_ref,
):
    k, v = k_ref[...], v_ref[...]
    same, crossed = same_ref[...], crossed_ref[...]
    length = length_ref[0, 0]
    allowed = (pos_k_ref[...] <= pos_q_ref[...]) & (pos_k_ref[...] < length)
    valid = (pos_q_ref[...] < length).astype(f32)
    grad_attended = (dot_nt(ga_ref[...], wo_ref[...]) * valid).astype(bf16)
    size = k.shape[1]
    grad_key = grad_value = 0.0
    for h in range(grad_attended.shape[1] // size):
        at = slice(h * size, (h + 1) * size)
        q, g = q_ref[:, at], grad_attended[:, at]
        probs = probabilities(q, k, allowed, scale)
        grad_probs = dot_nt(g, v)
        delta = jnp.sum(probs * grad_probs, axis=-1, keepdims=True)
        grad_scores = (probs * (grad_probs - delta)).astype(bf16)
        gq_ref[:, at] = rotate(dot(grad_scores, k) * scale, same, -crossed).astype(bf16)
        grad_key += dot_tn(grad_scores, q)
        grad_value += dot_tn(probs.astype(bf16), g)
    n = kept_ref.shape[0]
    for ref, at in ((kv_kept_ref, slice(0, n)), (kv_sent_ref, slice(n, 2 * n))):
        ref[:, :size] = grad_key[at] * scale
        ref[:, size:] = grad_value[at]
    sent_ref[...] = dot_nt(gq_ref[n:], wq_ref[...])
    kept_ref[...] = dot_nt(gq_ref[:n], wq_ref[...])


def pair_kernel(transposed, *refs):
    n = (len(refs) - 2) // 2
    kept, sent = refs[2 * n :]
    half = kept.shape[0]
    for out, at in ((sent, slice(half, 2 * half)), (kept, slice(0, half))):
        total = 0.0
        for rows, matrix in zip(refs[:n], refs[n : 2 * n]):
            total += (dot_nt if transposed else dot)(rows[at, :], matrix[...])
        out[...] = total


def pair_dots(name, rows, matrices, transposed, tile=512):
    count, depth = rows[0].shape
    width = matrices[0].shape[0 if transposed else 1]
    whole = pl.BlockSpec((count, depth), lambda t: (0, 0), pipeline_mode=pl.Buffered(1))
    part = pl.BlockSpec((tile, depth), lambda t: (t, 0)) if transposed else pl.BlockSpec((depth, tile), lambda t: (0, t))
    return pl.pallas_call(
        functools.partial(pair_kernel, transposed),
        grid=(width // tile,),
        in_specs=[whole] * len(rows) + [part] * len(matrices),
        out_specs=[pl.BlockSpec((count // 2, tile), lambda t: (0, t))] * 2,
        out_shape=[jax.ShapeDtypeStruct((count // 2, width), f32)] * 2,
        name=name,
        compiler_params=pltpu.CompilerParams(vmem_limit_bytes=48 * 2**20),
        cost_estimate=light,
    )(*rows, *matrices)


def out_kernel(places, left_ref, right_ref, out_ref):
    width = out_ref.shape[1] // GROUP
    for i in range(GROUP):
        at = pl.ds(pl.multiple_of(places[i] * width, width), width)
        out_ref[:, i * width : (i + 1) * width] = dot_tn(left_ref[...], right_ref[:, at])


def late_kernel(places, attended_ref, ga_ref, normed_ref, gq_ref, out_ref, sent_ref, kept_ref):
    width = out_ref.shape[1] // GROUP
    for i in range(GROUP):
        rows = slice(i * width, (i + 1) * width)
        sent = pl.ds(pl.multiple_of(places[i] * width, width), width)
        kept = pl.ds(pl.multiple_of(places[GROUP + i] * width, width), width)
        sent_ref[rows] = dot_tn(normed_ref[:, sent], gq_ref[...])
        kept_ref[rows] = dot_tn(normed_ref[:, kept], gq_ref[...])
        out_ref[:, rows] = dot_tn(attended_ref[...], ga_ref[:, kept])


def placed_call(kernel, name, places, ins, outs):
    def whole(shape):
        return pl.BlockSpec(shape, lambda t, p: (0,) * len(shape), pipeline_mode=pl.Buffered(1))

    return pl.pallas_call(
        kernel,
        grid_spec=pltpu.PrefetchScalarGridSpec(
            num_scalar_prefetch=1,
            grid=(1,),
            in_specs=[whole(a.shape) for a in ins],
            out_specs=[pl.BlockSpec(a.shape, lambda t, p: (0,) * len(a.shape)) for a in outs],
        ),
        out_shape=outs,
        name=name,
        compiler_params=pltpu.CompilerParams(vmem_limit_bytes=48 * 2**20),
        cost_estimate=light,
    )(places, *ins)


def rows_call(kernel, name, quarters, stacked, shared, outs, totals, tile=16, prefetch=()):
    count, width = quarters[0][0].shape
    args = [a for group in quarters for a in group] + list(stacked) + list(shared)
    specs = [pl.BlockSpec((tile, width), lambda t, *p: (t, 0))] * (4 * len(quarters))
    specs += [pl.BlockSpec((4, tile, a.shape[2]), lambda t, *p: (0, t, 0)) for a in stacked]
    specs += [pl.BlockSpec(a.shape, lambda t, *p: (0, 0)) for a in shared]
    out_specs = [pl.BlockSpec((4, tile, w), lambda t, *p: (0, t, 0)) for w, _ in outs]
    out_specs += [pl.BlockSpec((1, width), lambda t, *p: (0, 0))] * totals
    out_shape = [jax.ShapeDtypeStruct((4, count, w), kind) for w, kind in outs]
    out_shape += [jax.ShapeDtypeStruct((1, width), f32)] * totals
    return pl.pallas_call(
        kernel,
        grid_spec=pltpu.PrefetchScalarGridSpec(
            num_scalar_prefetch=len(prefetch), grid=(count // tile,), in_specs=specs, out_specs=out_specs
        ),
        out_shape=out_shape,
        name=name,
        compiler_params=pltpu.CompilerParams(vmem_limit_bytes=32 * 2**20),
        cost_estimate=light,
    )(*prefetch, *args)


def mid_kernel(places, *refs):
    hidden, (gain, out), picked = refs[:4], refs[4:6], refs[6:]
    for j in range(4):
        h = hidden[j][...]
        r = inverse_rms(h)
        out[j] = (h * r * gain[...]).astype(bf16)
        for part in range(2 * len(picked)):
            n = picked[0].shape[2] // 2
            at = pl.ds(pl.multiple_of(places[part] * n, n), n)
            picked[0][j, :, part * n : (part + 1) * n] = (hidden[j][:, at] * r * gain[:, at]).astype(bf16)


def mid_back_kernel(*refs):
    grads, hidden, (grad_out, gain, grad_hidden, rounded, total) = refs[:4], refs[4:8], refs[8:]
    gain = gain[...]
    acc = 0.0
    for j in range(4):
        h, g = hidden[j][...], grads[j][...]
        r = inverse_rms(h)
        acc += jnp.sum(g * h * r, axis=0, keepdims=True)
        back = grad_out[j].astype(f32) + norm_back(h, r, gain, g)
        grad_hidden[j] = back
        rounded[j] = back.astype(bf16)

    @pl.when(pl.program_id(0) == 0)
    def _():
        total[...] = jnp.zeros_like(total)

    total[...] += acc


def in_back_kernel(places, *refs):
    sums, (keyed, inputs, grad_hidden, gain, out, total) = refs[:4], refs[4:]
    gain = gain[...]
    acc = 0.0
    for j in range(4):
        stream = inputs[j].astype(f32)
        g = sums[j][...] + keyed[j]
        r = inverse_rms(stream)
        acc += jnp.sum(g * stream * r, axis=0, keepdims=True)
        out[places[j]] = (grad_hidden[j] + norm_back(stream, r, gain, g)).astype(bf16)

    @pl.when(pl.program_id(0) == 0)
    def _():
        total[...] = jnp.zeros_like(total)

    total[...] += acc


def add_kernel(places, *refs):
    left, right, (out,) = refs[:4], refs[4:8], refs[8:]
    for j in range(4):
        out[places[j]] = (left[j][...] + right[j][...]).astype(bf16)


def pack_kernel(n, places, *refs):
    blocks, scale, out, picked = refs[:n], refs[n], refs[n + 1], refs[n + 2]
    width = picked.shape[2] // 2
    for j in range(n):
        out[j] = (blocks[j][...] * scale[...]).astype(bf16)
        for part in range(2):
            at = pl.ds(pl.multiple_of(places[part] * width, width), width)
            picked[j, :, part * width : (part + 1) * width] = (blocks[j][:, at] * scale[:, at]).astype(bf16)


def pack(blocks, scale, places, rows, tile=32):
    n = len(blocks)
    count, width = blocks[0].shape
    block = pl.BlockSpec((tile, width), lambda t, places: (t, 0))
    out, picked = pl.pallas_call(
        functools.partial(pack_kernel, n),
        grid_spec=pltpu.PrefetchScalarGridSpec(
            num_scalar_prefetch=1,
            grid=(count // tile,),
            in_specs=[block] * n + [pl.BlockSpec((1, width), lambda t, places: (0, 0))],
            out_specs=[
                pl.BlockSpec((n, tile, width), lambda t, places: (0, t, 0)),
                pl.BlockSpec((n, tile, 2 * rows), lambda t, places: (0, t, 0)),
            ],
        ),
        out_shape=[
            jax.ShapeDtypeStruct((n, count, width), bf16),
            jax.ShapeDtypeStruct((n, count, 2 * rows), bf16),
        ],
        compiler_params=pltpu.CompilerParams(vmem_limit_bytes=32 * 2**20),
        cost_estimate=light,
    )(places, *blocks, scale.reshape(1, width))
    return out.reshape(n * count, width), picked.reshape(n * count, 2 * rows)


def ffn_kernel(own, has_prev, *refs):
    nm_ref, go_ref, nmc_ref, goc_ref, wg_ref, wu_ref, wd_ref = refs[:7]
    previous = refs[7:13] if has_prev else None
    outs = refs[13:] if has_prev else refs[7:]
    gate = dot(nm_ref[...], wg_ref[...])
    up = dot(nm_ref[...], wu_ref[...])
    grad_mixed = dot_nt(go_ref[...], wd_ref[...]).astype(bf16).astype(f32)
    sig = jax.nn.sigmoid(gate)
    gate_sig = gate * sig
    mixed = (gate_sig * up).astype(bf16)
    grad_gate = (grad_mixed * up * sig * (1.0 + gate * (1.0 - sig))).astype(bf16)
    grad_up = (grad_mixed * gate_sig).astype(bf16)
    n = nmc_ref.shape[1] // 2
    by_gate = dot_tn(nmc_ref[...], grad_gate)
    by_up = dot_tn(nmc_ref[...], grad_up)
    by_down = dot_tn(mixed, goc_ref[...])
    sums = (by_gate[:n], by_gate[n:], by_up[:n], by_up[n:], by_down[:, :n], by_down[:, n:])
    for i in range(6):
        outs[i][...] = sums[i] + previous[i][...] if has_prev else sums[i]
    if own:
        outs[6][...] = mixed
        outs[7][...] = grad_gate
        outs[8][...] = grad_up


def ffn(nm, go, nm_columns, go_columns, w_gate, w_up, w_down, previous=(), own=False, tile=512):
    count, width = nm.shape
    hidden = w_gate.shape[1]
    n = nm_columns.shape[1] // 2

    def whole(shape):
        return pl.BlockSpec(shape, lambda t: (0, 0), pipeline_mode=pl.Buffered(1))

    across = pl.BlockSpec((n, tile), lambda t: (0, t))
    down = pl.BlockSpec((tile, n), lambda t: (t, 0))
    sums = [across] * 4 + [down] * 2
    out_specs = list(sums)
    out_shape = [jax.ShapeDtypeStruct((n, hidden), f32)] * 4 + [jax.ShapeDtypeStruct((hidden, n), f32)] * 2
    if own:
        out_specs += [pl.BlockSpec((count, tile), lambda t: (0, t))] * 3
        out_shape += [jax.ShapeDtypeStruct((count, hidden), bf16)] * 3
    columns = pl.BlockSpec((width, tile), lambda t: (0, t))
    in_specs = [whole(nm.shape), whole(go.shape), whole(nm_columns.shape), whole(go_columns.shape)]
    in_specs += [columns, columns, pl.BlockSpec((tile, width), lambda t: (t, 0))]
    in_specs += sums if previous else []
    return pl.pallas_call(
        functools.partial(ffn_kernel, own, bool(previous)),
        grid=(pl.cdiv(hidden, tile),),
        in_specs=in_specs,
        out_specs=out_specs,
        out_shape=out_shape,
        compiler_params=pltpu.CompilerParams(vmem_limit_bytes=56 * 2**20),
        cost_estimate=light,
    )(nm, go, nm_columns, go_columns, w_gate, w_up, w_down, *previous)


def shards(
    sizes,
    inputs,
    seq_lengths,
    norm_in,
    w_query,
    w_key,
    w_value,
    w_out,
    norm_mid,
    w_gate,
    w_up,
    w_down,
    out_cotangent,
    kv_cotangent,
):
    n_outer, n_dp = sizes
    seq_len, width = inputs.shape
    half, quarter = seq_len // 2, seq_len // 4
    head = w_key.shape[1]
    own_heads = w_query.shape[1]
    scale = head ** (-0.5)
    rows = width // n_dp
    z, x = lax.axis_index("z"), lax.axis_index("x")
    order = Order()
    run, swap, wait = order.run, order.swap, order.wait
    one = jnp.minimum(seq_lengths[0], 1).astype(f32)
    me = 2 * lax.axis_index("c") + lax.axis_index("y")
    quarters = jnp.stack([me ^ k for k in range(4)]).astype(jnp.int32)
    others = [lax.rem(z + k, GROUP) for k in range(1, GROUP)]
    places = jnp.stack([2 * z + 1 - x, 2 * z + x, *others]).astype(jnp.int32)
    positions = (quarters[:, None] * quarter + jnp.arange(quarter, dtype=jnp.int32)[None, :]).reshape(seq_len)
    gain_in, gain_mid = norm_in.reshape(1, width), norm_mid.reshape(1, width)
    ones = jnp.ones_like(norm_mid)
    same, crossed = rotary_tables(positions, head)
    masks = (same, crossed, positions[:, None], positions[None, :], seq_lengths.reshape(1, 1))
    weights = (w_gate, w_up, w_down)

    def shape(n, kind, count=seq_len):
        return jax.ShapeDtypeStruct((count, n), kind)

    def scaled(block):
        return block * inverse_rms(block)

    def remote(gathered):
        return [lax.dynamic_index_in_dim(gathered, k, 0, keepdims=False) for k in others]

    def columns(part):
        part = part.reshape(part.shape[0], n_outer, GROUP, 2, rows) if n_outer > 1 else part
        taken = []
        for which in (1 - x, x):
            if n_outer > 1:
                cut = lax.dynamic_index_in_dim(part, z, 2, keepdims=False)
                cut = lax.dynamic_index_in_dim(cut, which, 2, keepdims=False)
                taken.append(cut.reshape(part.shape[0], n_outer * rows))
            else:
                taken.append(lax.dynamic_slice_in_dim(part, (2 * z + which) * rows, rows, 1))
        return jnp.concatenate(taken, axis=1)

    def packed_z(own, far, gain):
        if n_outer == 1:
            return run(lambda own, far: pack_z(own, far, gain, places, rows), own, far)
        return packed(remote(own), remote(far), gain)

    def packed(blocks, far, gain):
        blocks = [*blocks, *far]
        if n_outer == 1:
            return run(lambda *blocks: pack(blocks, gain, places, rows), *blocks)
        whole = run(lambda *blocks: (jnp.concatenate(blocks, axis=0) * (gain * one)).astype(bf16), *blocks)
        return whole, columns(whole)

    def add_y(kept, received):
        return kept[:quarter] + received

    def wgrads(*args):
        return ffn(*args[:4], *weights, previous=args[4:])

    inputs, grad_down_in, kv_cotangent, go_quarter = run(
        arrange, quarters, seq_lengths, inputs, out_cotangent, kv_cotangent
    )
    go_z = lax.all_gather(go_quarter, "z", axis=0, tiled=False)

    kept, sent, normed, queries, key_rot, value_rows, attended = run(
        lambda *args: call(
            functools.partial(forward_kernel, scale),
            "attention_forward",
            args,
            [shape(width, f32, half), shape(width, f32, half), shape(width, bf16), shape(own_heads, bf16),
             shape(head, bf16), shape(head, bf16), shape(own_heads, bf16)],
        ),
        inputs, gain_in, w_query, w_key, w_value, w_out, *masks,
    )
    sent = swap(sent, "c")
    go_own_columns = run(columns, grad_down_in)
    kept = run(jnp.add, kept, sent)
    received = swap(kept[quarter:], "y")

    def hidden_of(kept, received, inputs):
        own = add_y(kept, received) + inputs.astype(f32)
        return own, scaled(own)

    own, scaled_own = run(hidden_of, kept, received, inputs[:quarter])
    nm_z_own = lax.all_gather(scaled_own, "z", axis=0, tiled=False)
    other = swap(own, "y")
    far_own = swap(own, "c")
    go_remote = run(remote, go_z)
    scaled_other = run(scaled, other)
    nm_z_other = lax.all_gather(scaled_other, "z", axis=0, tiled=False)
    far_other = swap(other, "c")
    hidden = [own, other, far_own, far_other]

    picked = [(2 * rows, bf16)] if n_outer == 1 else []
    normed_mid, *nm_own_columns = run(
        lambda *hidden: rows_call(
            mid_kernel, "mid_norm", [hidden], [], [gain_mid], [(width, bf16), *picked], 0, prefetch=(places,)
        ),
        *hidden,
    )
    normed_mid = normed_mid.reshape(seq_len, width)
    nm_own_columns = nm_own_columns[0].reshape(seq_len, 2 * rows) if n_outer == 1 else columns(normed_mid)
    go_other = [swap(go_remote[0], "y")]
    *sums, mixed, grad_gate, grad_up = run(
        lambda *args: ffn(*args, *weights, own=True),
        normed_mid, grad_down_in, nm_own_columns, go_own_columns,
    )
    go_other[0] = wait(go_other[0])
    mid_kept, mid_sent = run(
        lambda *args: pair_dots("mid_part", args[:2], args[2:], True), grad_gate, grad_up, w_gate, w_up
    )
    mid_sent = swap(mid_sent, "c")
    kept = run(jnp.add, mid_kept, mid_sent)
    received = swap(kept[quarter:], "y")
    own = run(add_y, kept, received)
    other = swap(own, "y")
    nm_z_own = wait(nm_z_own)
    far_own = swap(own, "c")
    go_far, nm_far = swap(go_z, "c"), swap(nm_z_own, "c")
    down_kept, down_sent = run(lambda *args: pair_dots("down_part", args[:1], args[1:], False), mixed, w_down)
    down_sent = swap(down_sent, "c")
    go, go_columns = packed_z(go_z, go_far, ones)
    nm, nm_columns = packed_z(nm_z_own, nm_far, norm_mid)
    other = wait(other)
    go_other += [order.move(block, "y", [(0, 1), (1, 0)], queue=False) for block in go_remote[1:]]
    grad_mid = [own, other, far_own, swap(other, "c")]
    grad_hidden, grad_attention, grad_norm_mid = run(
        lambda *args: rows_call(
            mid_back_kernel, "mid_back", [args[:4], args[4:]], [grad_down_in.reshape(4, quarter, width)], [gain_mid],
            [(width, f32), (width, bf16)], 1,
        ),
        *grad_mid, *hidden,
    )
    grad_attention = grad_attention.reshape(seq_len, width)

    if n_outer == 1:
        at_x = 2 * jnp.arange(GROUP, dtype=jnp.int32)
        at_x = jnp.concatenate([at_x + 1 - x, at_x + x])
        (out_sent,) = run(
            lambda *args: placed_call(out_kernel, "out_grad", at_x, args, [shape(width // 2, f32, own_heads)]),
            attended, grad_attention,
        )
    else:
        out_sent = run(dot_tn, attended, by_x(grad_attention, 1 - x, rows))
    out_sent = swap(out_sent, "x")
    kept, sent, kv_kept, kv_sent, grad_query = run(
        lambda *args: call(
            functools.partial(backward_kernel, scale),
            "attention_backward",
            args,
            [shape(width, f32, half), shape(width, f32, half), shape(2 * head, f32, half), shape(2 * head, f32, half),
             shape(own_heads, bf16)],
        ),
        grad_attention, w_out, w_query, queries, key_rot, value_rows, *masks,
    )
    sent = swap(sent, "c")
    kv_sent = swap(kv_sent, "c")
    if n_outer == 1:
        out_kept, query_sent, query_kept = run(
            lambda *args: placed_call(
                late_kernel, "late_grads", at_x, args,
                [shape(width // 2, f32, own_heads), shape(own_heads, f32, width // 2), shape(own_heads, f32, width // 2)],
            ),
            attended, grad_attention, normed, grad_query,
        )
    else:
        out_kept = run(dot_tn, attended, by_x(grad_attention, x, rows))
        query_sent = run(dot_tn, by_x(normed, 1 - x, rows), grad_query)
        query_kept = run(dot_tn, by_x(normed, x, rows), grad_query)

    query_sent = order.move(query_sent, "x", [(0, 1), (1, 0)], queue=False)

    sums = run(wgrads, nm, go, nm_columns, go_columns, *sums)
    go_other[1:] = [wait(block) for block in go_other[1:]]
    out_half = run(jnp.add, out_kept, out_sent)
    if n_outer == 1:
        out_kept, out_sent = run(lambda a: split(a, 1, z // 2), out_half)
        out_sent = order.pair_z(out_sent, 2)
    nm_z_other = wait(nm_z_other)
    go_far = [swap(block, "c") for block in go_other]
    nm_far = swap(nm_z_other, "c")
    kept = run(jnp.add, kept, sent)
    received = swap(kept[quarter:], "y")
    kv_kept = run(jnp.add, kv_kept, kv_sent)
    kv_received = order.move(kv_kept[quarter:], "y", [(0, 1), (1, 0)], queue=False)
    down_kept = run(jnp.add, down_kept, down_sent)
    go, go_columns = packed(go_other, go_far, ones)
    nm, nm_columns = packed_z(nm_z_other, nm_far, norm_mid)
    sums = run(wgrads, nm, go, nm_columns, go_columns, *sums)
    gate_sent = swap(sums[0], "x")
    summed_own = run(add_y, kept, received)
    summed_other = swap(summed_own, "y")
    kv_own = run(add_y, kv_kept, kv_received)
    kv_other = order.move(kv_own, "y", [(0, 1), (1, 0)], queue=False)
    if n_outer == 1:
        out_half = run(jnp.add, out_kept, out_sent)
        out_kept, out_sent = run(lambda a: split(a, 1, z % 2), out_half)
        out_sent = order.pair_z(out_sent, 1)
    query_half = run(jnp.add, query_kept, query_sent)
    if n_outer == 1:
        query_kept, query_sent = run(lambda a: split(a, 0, z // 2), query_half)
        query_sent = order.pair_z(query_sent, 2)
    grad_w_gate = run(jnp.add, sums[1], gate_sent)
    up_sent = swap(sums[2], "x")

    summed_other = wait(summed_other)
    down_received = swap(down_kept[quarter:], "y")
    far = [swap(a, "c") for a in (kv_own, kv_other, summed_own, summed_other)]

    def key_value(*parts):
        grad_kv = jnp.concatenate(parts, axis=0) + kv_cotangent
        grad_key = grad_kv[:, :head]
        crossed_key = jnp.concatenate([grad_key[:, head // 2 :], grad_key[:, : head // 2]], axis=1)
        return (grad_key * same - crossed_key * crossed).astype(bf16), grad_kv[:, head:].astype(bf16)

    grad_key, grad_value = run(key_value, kv_own, kv_other, far[0], far[1])
    keyed = run(lambda k, v: dot_nt(k, w_key) + dot_nt(v, w_value), grad_key, grad_value)
    grad_inputs, grad_norm_in = run(
        lambda keyed, *summed: rows_call(
            in_back_kernel, "in_back", [summed],
            [keyed.reshape(4, quarter, width), inputs.reshape(4, quarter, width), grad_hidden], [gain_in],
            [(width, bf16)], 1, prefetch=(quarters,),
        ),
        keyed, summed_own, summed_other, far[2], far[3],
    )

    piece = rows // 4
    m = 2 * lax.axis_index("y") + lax.axis_index("c")

    def small_sums(grad_key, grad_value, grad_norm_in, grad_norm_mid):
        kv = jnp.concatenate([dot_tn(normed, grad_key), dot_tn(normed, grad_value)], axis=1)
        kv = lax.dynamic_index_in_dim(kv.reshape(n_dp, 4, piece, 2 * head), m, 1, keepdims=False)
        gains = jnp.concatenate([grad_norm_in, grad_norm_mid]).reshape(2, n_dp, rows).transpose(1, 0, 2)
        gains = jnp.pad(gains, ((0, 0), (0, 6), (0, 2 * head - rows)))
        small = jnp.concatenate([kv, gains], axis=1).reshape(n_dp // 2, 2, -1, 2 * head)
        return split(small, 1, x)

    small, small_sent = run(small_sums, grad_key, grad_value, grad_norm_in, grad_norm_mid)
    small_sent = order.move(small_sent, "x", [(0, 1), (1, 0)], queue=False)
    down_own = run(add_y, down_kept, down_received)
    down_other = swap(down_own, "y")
    small = run(jnp.add, small, small_sent).reshape(n_dp // 2, -1, 2 * head)
    if n_outer == 1:
        grad_w_out = run(jnp.add, out_kept, out_sent)
        small, small_sent = run(lambda a: split(a, 0, z // 2), small)
        small_sent = order.move(small_sent, "z", [(i, i ^ 2) for i in range(GROUP)], queue=False)
        small = run(jnp.add, small, small_sent)
        small, small_sent = run(lambda a: split(a, 0, z % 2), small)
        small_sent = order.move(small_sent, "z", [(i, i ^ 1) for i in range(GROUP)], queue=False)
    else:
        small = lax.psum_scatter(small, ("o", "z"), scatter_dimension=0, tiled=True)
        grad_w_out = lax.psum_scatter(out_half, ("o", "z"), scatter_dimension=1, tiled=True)
    grad_w_up = run(jnp.add, sums[3], up_sent)
    last_sent = swap(sums[4], "x")
    if n_outer == 1:
        small = run(jnp.add, small, small_sent)
        query_half = run(jnp.add, query_kept, query_sent)
        query_kept, query_sent = run(lambda a: split(a, 0, z % 2), query_half)
        query_sent = order.pair_z(query_sent, 1)
    kv = run(lambda a: lax.all_gather(a[0, :piece], ("y", "c"), axis=0, tiled=True), small)
    out_norm_in, out_norm_mid = small[0, piece, :rows], small[0, piece + 1, :rows]

    down_other = wait(down_other)
    down = [down_own, down_other, swap(down_own, "c"), swap(down_other, "c")]
    (result,) = run(
        lambda *args: rows_call(
            add_kernel, "result", [args[:4], args[4:]], [], [], [(width, bf16)], 0, prefetch=(quarters,)
        ),
        *down, *hidden,
    )
    if n_outer == 1:
        grad_w_query = run(jnp.add, query_kept, query_sent)
    else:
        grad_w_query = lax.psum_scatter(query_half, ("o", "z"), scatter_dimension=0, tiled=True)
    grad_w_down = run(jnp.add, sums[5], last_sent)
    if n_outer > 1:
        grad_w_down = lax.psum_scatter(grad_w_down, "o", scatter_dimension=1, tiled=True)
        grad_w_gate = lax.psum_scatter(grad_w_gate, "o", scatter_dimension=0, tiled=True)
        grad_w_up = lax.psum_scatter(grad_w_up, "o", scatter_dimension=0, tiled=True)

    return (
        result.reshape(seq_len, width),
        grad_inputs.reshape(seq_len, width),
        out_norm_in,
        grad_w_query,
        kv[:, :head],
        kv[:, head:],
        grad_w_out,
        out_norm_mid,
        grad_w_gate,
        grad_w_up,
        grad_w_down,
    )


def solution(mesh):
    n_dp = mesh.shape["dp"]
    n_outer = n_dp // (2 * GROUP)
    split = Mesh(mesh.devices.reshape(n_outer, GROUP, 2, 2, 2), ("o", "z", "x", "y", "c"))
    dp, mp = ("o", "z", "x"), ("y", "c")

    def program(*args):
        return shards((n_outer, n_dp), *args)

    return jax.shard_map(
        program,
        mesh=split,
        in_specs=(
            P(dp, None),
            P(dp),
            P(),
            P(None, mp),
            P(),
            P(),
            P(mp, None),
            P(),
            P(None, mp),
            P(None, mp),
            P(mp, None),
            P(dp, None),
            P(dp, None),
        ),
        out_specs=(
            P(dp, None),
            P(dp, None),
            P(dp),
            P(dp, mp),
            P(dp, None),
            P(dp, None),
            P(mp, dp),
            P(dp),
            P(dp, mp),
            P(dp, mp),
            P(mp, dp),
        ),
        check_vma=False,
    )
```

```python
import functools

import jax
import jax.numpy as jnp
from jax import lax
from jax.experimental import pallas as pl
from jax.experimental.pallas import tpu as pltpu
from jax.sharding import Mesh, PartitionSpec as P

epsilon = 1e-06
masked_value = -1e30
GROUP = 4
f32 = jnp.float32
bf16 = jnp.bfloat16

light = pl.CostEstimate(flops=1, bytes_accessed=1, transcendentals=0)


def dot(a, b):
    return jnp.dot(a, b, preferred_element_type=f32)


def dot_nt(a, b):
    return lax.dot_general(a, b, (((1,), (1,)), ((), ())), preferred_element_type=f32)


def dot_tn(a, b):
    return lax.dot_general(a, b, (((0,), (0,)), ((), ())), preferred_element_type=f32)


def arrange_kernel(places, length_ref, inputs_ref, cotangent_ref, kv_ref, inputs_out, cotangent_out, kv_out, quarter_out):
    k = pl.program_id(0)
    count = inputs_ref.shape[0]
    row = lax.broadcasted_iota(jnp.int32, (count, 1), 0) + places[k] * count
    valid = row < length_ref[0, 0]
    inputs_out[...] = inputs_ref[...]
    cotangent = jnp.where(valid, cotangent_ref[...].astype(f32), 0.0)
    cotangent_out[...] = cotangent.astype(bf16)
    kv_out[...] = jnp.where(valid, kv_ref[...].astype(f32), 0.0)

    @pl.when(k == 0)
    def _():
        quarter_out[...] = cotangent


def arrange(places, lengths, inputs, cotangent, kv):
    seq_len, width = inputs.shape
    q = seq_len // 4
    kv_width = kv.shape[1]
    picked = pl.BlockSpec((q, width), lambda k, p: (p[k], 0))
    placed = pl.BlockSpec((q, width), lambda k, p: (k, 0))
    return pl.pallas_call(
        arrange_kernel,
        grid_spec=pltpu.PrefetchScalarGridSpec(
            num_scalar_prefetch=1,
            grid=(4,),
            in_specs=[
                pl.BlockSpec((1, 1), lambda k, p: (0, 0)),
                picked,
                picked,
                pl.BlockSpec((q, kv_width), lambda k, p: (p[k], 0)),
            ],
            out_specs=[
                placed,
                placed,
                pl.BlockSpec((q, kv_width), lambda k, p: (k, 0)),
                pl.BlockSpec((q, width), lambda k, p: (0, 0)),
            ],
        ),
        out_shape=[
            jax.ShapeDtypeStruct((seq_len, width), bf16),
            jax.ShapeDtypeStruct((seq_len, width), bf16),
            jax.ShapeDtypeStruct((seq_len, kv_width), f32),
            jax.ShapeDtypeStruct((q, width), f32),
        ],
        name="arrange",
        compiler_params=pltpu.CompilerParams(vmem_limit_bytes=32 * 2**20),
        cost_estimate=light,
    )(places, lengths.reshape(1, 1), inputs, cotangent, kv)


def rotary_tables(positions, size):
    half_size = size // 2
    inverse = 10000.0 ** (-2.0 * jnp.arange(half_size, dtype=f32) / size)
    angles = positions.astype(f32)[:, None] * inverse[None, :]
    cosine, sine = jnp.cos(angles), jnp.sin(angles)
    return jnp.concatenate([cosine, cosine], axis=1), jnp.concatenate([-sine, sine], axis=1)


def rotate(values, same, crossed):
    return values * same + pltpu.roll(values, values.shape[-1] // 2, 1) * crossed


def norm_back(stream, inverse_rms, gain, grad_normed):
    weighted = gain * grad_normed
    return inverse_rms * weighted - stream * inverse_rms**3 * jnp.mean(weighted * stream, axis=-1, keepdims=True)


def inverse_rms(block):
    return lax.rsqrt(jnp.mean(block * block, axis=-1, keepdims=True) + epsilon)


def pack_kernel(n, places, *refs):
    blocks, (scale, out, picked) = refs[:n], refs[n:]
    width = picked.shape[2] // 2
    for j in range(n):
        out[j] = (blocks[j][0] * scale[...]).astype(bf16)
        for part in range(2):
            at = pl.ds(pl.multiple_of(places[part] * width, width), width)
            picked[j, :, part * width : (part + 1) * width] = (blocks[j][0, :, at] * scale[:, at]).astype(bf16)


def pack(blocks, scale, places, rows, tile=32):
    count, width = blocks[0].shape[1:]
    args, specs = [], []
    for a in blocks:
        for k in range(GROUP - 1 if a.shape[0] == GROUP else a.shape[0]):
            args.append(a)
            if a.shape[0] == GROUP:
                specs.append(pl.BlockSpec((1, tile, width), lambda t, p, k=k: (p[2 + k], t, 0)))
            else:
                specs.append(pl.BlockSpec((1, tile, width), lambda t, p, k=k: (k, t, 0)))
    n = len(args)
    out, picked = pl.pallas_call(
        functools.partial(pack_kernel, n),
        grid_spec=pltpu.PrefetchScalarGridSpec(
            num_scalar_prefetch=1,
            grid=(count // tile,),
            in_specs=specs + [pl.BlockSpec((1, width), lambda t, p: (0, 0))],
            out_specs=[
                pl.BlockSpec((n, tile, width), lambda t, p: (0, t, 0)),
                pl.BlockSpec((n, tile, 2 * rows), lambda t, p: (0, t, 0)),
            ],
        ),
        out_shape=[
            jax.ShapeDtypeStruct((n, count, width), bf16),
            jax.ShapeDtypeStruct((n, count, 2 * rows), bf16),
        ],
        name="pack",
        compiler_params=pltpu.CompilerParams(vmem_limit_bytes=32 * 2**20),
        cost_estimate=light,
    )(places, *args, scale.reshape(1, width))
    return out.reshape(n * count, width), picked.reshape(n * count, 2 * rows)


class Order:
    def __init__(self):
        self.core = ()
        self.links = {}

    def run(self, f, *args):
        n = len(args)
        args = lax.optimization_barrier((*args, *self.core))[:n]
        outs = f(*args)
        self.core = tuple(outs)[:1] if isinstance(outs, (list, tuple)) else (outs,)
        return outs

    def wait(self, a):
        (a,) = self.run(lambda a: lax.optimization_barrier((a,)), a)
        return a

    def move(self, a, axis, pairs, queue=True):
        before = self.links.get(axis, ()) if queue else ()
        a = lax.optimization_barrier((a, *self.core, *before))[0]
        a = lax.ppermute(a, axis, pairs)
        if queue:
            self.links[axis] = (a,)
        return a

    def swap(self, a, axis):
        return self.move(a, axis, [(0, 1), (1, 0)], queue=axis != "c")

    def pair_z(self, a, bit):
        return self.move(a, "z", [(i, i ^ bit) for i in range(GROUP)])


def split(a, axis, mine):
    n = a.shape[axis] // 2
    return lax.dynamic_slice_in_dim(a, mine * n, n, axis), lax.dynamic_slice_in_dim(a, (1 - mine) * n, n, axis)


def by_x(a, which, rows):
    n = a.shape[1] // (2 * rows)
    return jnp.concatenate([lax.dynamic_slice_in_dim(a, (2 * i + which) * rows, rows, 1) for i in range(n)], axis=1)


def call(kernel, name, ins, outs):
    return pl.pallas_call(
        kernel,
        out_shape=outs,
        name=name,
        compiler_params=pltpu.CompilerParams(vmem_limit_bytes=56 * 2**20),
        cost_estimate=light,
    )(*ins)


def probabilities(q, k, allowed, scale):
    scores = jnp.where(allowed, dot_nt(q, k) * scale, masked_value)
    exponent = jnp.exp(scores - jnp.max(scores, axis=-1, keepdims=True))
    return exponent / jnp.sum(exponent, axis=-1, keepdims=True)


def forward_kernel(
    scale, x_ref, gain_ref, wq_ref, wk_ref, wv_ref, wo_ref, same_ref, crossed_ref, pos_q_ref, pos_k_ref, length_ref,
    kept_ref, sent_ref, normed_ref, q_ref, k_ref, v_ref, attended_ref,
):
    stream = x_ref[...].astype(f32)
    normed_ref[...] = (stream * inverse_rms(stream) * gain_ref[...]).astype(bf16)
    normed = normed_ref[...]
    same, crossed = same_ref[...], crossed_ref[...]
    k = rotate(dot(normed, wk_ref[...]), same, crossed).astype(bf16)
    v = dot(normed, wv_ref[...]).astype(bf16)
    k_ref[...], v_ref[...] = k, v
    raw = dot(normed, wq_ref[...])
    length = length_ref[0, 0]
    allowed = (pos_k_ref[...] <= pos_q_ref[...]) & (pos_k_ref[...] < length)
    valid = (pos_q_ref[...] < length).astype(f32)
    size = k.shape[1]
    for h in range(raw.shape[1] // size):
        at = slice(h * size, (h + 1) * size)
        q = rotate(raw[:, at], same, crossed).astype(bf16)
        q_ref[:, at] = q
        weights = probabilities(q, k, allowed, scale).astype(bf16)
        attended_ref[:, at] = (dot(weights, v) * valid).astype(bf16)
    n = kept_ref.shape[0]
    sent_ref[...] = dot(attended_ref[n:], wo_ref[...])
    kept_ref[...] = dot(attended_ref[:n], wo_ref[...])


def backward_kernel(
    scale, ga_ref, wo_ref, wq_ref, q_ref, k_ref, v_ref, same_ref, crossed_ref, pos_q_ref, pos_k_ref, length_ref,
    kept_ref, sent_ref, kv_kept_ref, kv_sent_ref, gq_ref,
):
    k, v = k_ref[...], v_ref[...]
    same, crossed = same_ref[...], crossed_ref[...]
    length = length_ref[0, 0]
    allowed = (pos_k_ref[...] <= pos_q_ref[...]) & (pos_k_ref[...] < length)
    valid = (pos_q_ref[...] < length).astype(f32)
    grad_attended = (dot_nt(ga_ref[...], wo_ref[...]) * valid).astype(bf16)
    size = k.shape[1]
    grad_key = grad_value = 0.0
    for h in range(grad_attended.shape[1] // size):
        at = slice(h * size, (h + 1) * size)
        q, g = q_ref[:, at], grad_attended[:, at]
        probs = probabilities(q, k, allowed, scale)
        grad_probs = dot_nt(g, v)
        delta = jnp.sum(probs * grad_probs, axis=-1, keepdims=True)
        grad_scores = (probs * (grad_probs - delta)).astype(bf16)
        gq_ref[:, at] = rotate(dot(grad_scores, k) * scale, same, -crossed).astype(bf16)
        grad_key += dot_tn(grad_scores, q)
        grad_value += dot_tn(probs.astype(bf16), g)
    n = kept_ref.shape[0]
    for ref, at in ((kv_kept_ref, slice(0, n)), (kv_sent_ref, slice(n, 2 * n))):
        ref[:, :size] = grad_key[at] * scale
        ref[:, size:] = grad_value[at]
    sent_ref[...] = dot_nt(gq_ref[n:], wq_ref[...])
    kept_ref[...] = dot_nt(gq_ref[:n], wq_ref[...])


def pair_kernel(transposed, *refs):
    n = (len(refs) - 2) // 2
    kept, sent = refs[2 * n :]
    half = kept.shape[0]
    for out, at in ((sent, slice(half, 2 * half)), (kept, slice(0, half))):
        total = 0.0
        for rows, matrix in zip(refs[:n], refs[n : 2 * n]):
            total += (dot_nt if transposed else dot)(rows[at, :], matrix[...])
        out[...] = total


def pair_dots(name, rows, matrices, transposed, tile=512):
    count, depth = rows[0].shape
    width = matrices[0].shape[0 if transposed else 1]
    whole = pl.BlockSpec((count, depth), lambda t: (0, 0), pipeline_mode=pl.Buffered(1))
    part = pl.BlockSpec((tile, depth), lambda t: (t, 0)) if transposed else pl.BlockSpec((depth, tile), lambda t: (0, t))
    return pl.pallas_call(
        functools.partial(pair_kernel, transposed),
        grid=(width // tile,),
        in_specs=[whole] * len(rows) + [part] * len(matrices),
        out_specs=[pl.BlockSpec((count // 2, tile), lambda t: (0, t))] * 2,
        out_shape=[jax.ShapeDtypeStruct((count // 2, width), f32)] * 2,
        name=name,
        compiler_params=pltpu.CompilerParams(vmem_limit_bytes=48 * 2**20),
        cost_estimate=light,
    )(*rows, *matrices)


def out_kernel(places, left_ref, right_ref, out_ref):
    width = out_ref.shape[1] // GROUP
    for i in range(GROUP):
        at = pl.ds(pl.multiple_of(places[i] * width, width), width)
        out_ref[:, i * width : (i + 1) * width] = dot_tn(left_ref[...], right_ref[:, at])


def late_kernel(places, attended_ref, ga_ref, normed_ref, gq_ref, out_ref, sent_ref, kept_ref):
    width = out_ref.shape[1] // GROUP
    for i in range(GROUP):
        rows = slice(i * width, (i + 1) * width)
        sent = pl.ds(pl.multiple_of(places[i] * width, width), width)
        kept = pl.ds(pl.multiple_of(places[GROUP + i] * width, width), width)
        sent_ref[rows] = dot_tn(normed_ref[:, sent], gq_ref[...])
        kept_ref[rows] = dot_tn(normed_ref[:, kept], gq_ref[...])
        out_ref[:, rows] = dot_tn(attended_ref[...], ga_ref[:, kept])


def placed_call(kernel, name, places, ins, outs):
    def whole(shape):
        return pl.BlockSpec(shape, lambda t, p: (0,) * len(shape), pipeline_mode=pl.Buffered(1))

    return pl.pallas_call(
        kernel,
        grid_spec=pltpu.PrefetchScalarGridSpec(
            num_scalar_prefetch=1,
            grid=(1,),
            in_specs=[whole(a.shape) for a in ins],
            out_specs=[pl.BlockSpec(a.shape, lambda t, p: (0,) * len(a.shape)) for a in outs],
        ),
        out_shape=outs,
        name=name,
        compiler_params=pltpu.CompilerParams(vmem_limit_bytes=48 * 2**20),
        cost_estimate=light,
    )(places, *ins)


def rows_call(kernel, name, quarters, stacked, shared, outs, totals, tile=16, prefetch=()):
    count, width = quarters[0][0].shape
    args = [a for group in quarters for a in group] + list(stacked) + list(shared)
    specs = [pl.BlockSpec((tile, width), lambda t, *p: (t, 0))] * (4 * len(quarters))
    specs += [pl.BlockSpec((4, tile, a.shape[2]), lambda t, *p: (0, t, 0)) for a in stacked]
    specs += [pl.BlockSpec(a.shape, lambda t, *p: (0, 0)) for a in shared]
    out_specs = [pl.BlockSpec((4, tile, w), lambda t, *p: (0, t, 0)) for w, _ in outs]
    out_specs += [pl.BlockSpec((1, width), lambda t, *p: (0, 0))] * totals
    out_shape = [jax.ShapeDtypeStruct((4, count, w), kind) for w, kind in outs]
    out_shape += [jax.ShapeDtypeStruct((1, width), f32)] * totals
    return pl.pallas_call(
        kernel,
        grid_spec=pltpu.PrefetchScalarGridSpec(
            num_scalar_prefetch=len(prefetch), grid=(count // tile,), in_specs=specs, out_specs=out_specs
        ),
        out_shape=out_shape,
        name=name,
        compiler_params=pltpu.CompilerParams(vmem_limit_bytes=32 * 2**20),
        cost_estimate=light,
    )(*prefetch, *args)


def mid_kernel(places, *refs):
    hidden, (gain, out), picked = refs[:4], refs[4:6], refs[6:]
    for j in range(4):
        h = hidden[j][...]
        r = inverse_rms(h)
        out[j] = (h * r * gain[...]).astype(bf16)
        for part in range(2 * len(picked)):
            n = picked[0].shape[2] // 2
            at = pl.ds(pl.multiple_of(places[part] * n, n), n)
            picked[0][j, :, part * n : (part + 1) * n] = (hidden[j][:, at] * r * gain[:, at]).astype(bf16)


def mid_back_kernel(*refs):
    grads, hidden, (grad_out, gain, grad_hidden, rounded, total) = refs[:4], refs[4:8], refs[8:]
    gain = gain[...]
    acc = 0.0
    for j in range(4):
        h, g = hidden[j][...], grads[j][...]
        r = inverse_rms(h)
        acc += jnp.sum(g * h * r, axis=0, keepdims=True)
        back = grad_out[j].astype(f32) + norm_back(h, r, gain, g)
        grad_hidden[j] = back
        rounded[j] = back.astype(bf16)

    @pl.when(pl.program_id(0) == 0)
    def _():
        total[...] = jnp.zeros_like(total)

    total[...] += acc


def in_back_kernel(places, *refs):
    sums, (keyed, inputs, grad_hidden, gain, out, total) = refs[:4], refs[4:]
    gain = gain[...]
    acc = 0.0
    for j in range(4):
        stream = inputs[j].astype(f32)
        g = sums[j][...] + keyed[j]
        r = inverse_rms(stream)
        acc += jnp.sum(g * stream * r, axis=0, keepdims=True)
        out[places[j]] = (grad_hidden[j] + norm_back(stream, r, gain, g)).astype(bf16)

    @pl.when(pl.program_id(0) == 0)
    def _():
        total[...] = jnp.zeros_like(total)

    total[...] += acc


def add_kernel(places, *refs):
    left, right, (out,) = refs[:4], refs[4:8], refs[8:]
    for j in range(4):
        out[places[j]] = (left[j][...] + right[j][...]).astype(bf16)


def ffn_kernel(own, has_prev, *refs):
    nm_ref, go_ref, nmc_ref, goc_ref, wg_ref, wu_ref, wd_ref = refs[:7]
    previous = refs[7:13] if has_prev else None
    outs = refs[13:] if has_prev else refs[7:]
    gate = dot(nm_ref[...], wg_ref[...])
    up = dot(nm_ref[...], wu_ref[...])
    grad_mixed = dot_nt(go_ref[...], wd_ref[...]).astype(bf16).astype(f32)
    sig = jax.nn.sigmoid(gate)
    gate_sig = gate * sig
    mixed = (gate_sig * up).astype(bf16)
    grad_gate = (grad_mixed * up * sig * (1.0 + gate * (1.0 - sig))).astype(bf16)
    grad_up = (grad_mixed * gate_sig).astype(bf16)
    n = nmc_ref.shape[1] // 2
    by_gate = dot_tn(nmc_ref[...], grad_gate)
    by_up = dot_tn(nmc_ref[...], grad_up)
    by_down = dot_tn(mixed, goc_ref[...])
    sums = (by_gate[:n], by_gate[n:], by_up[:n], by_up[n:], by_down[:, :n], by_down[:, n:])
    for i in range(6):
        outs[i][...] = sums[i] + previous[i][...] if has_prev else sums[i]
    if own:
        outs[6][...] = mixed
        outs[7][...] = grad_gate
        outs[8][...] = grad_up


def ffn(nm, go, nm_columns, go_columns, w_gate, w_up, w_down, previous=(), own=False, tile=512):
    count, width = nm.shape
    hidden = w_gate.shape[1]
    n = nm_columns.shape[1] // 2

    def whole(shape):
        return pl.BlockSpec(shape, lambda t: (0, 0), pipeline_mode=pl.Buffered(1))

    across = pl.BlockSpec((n, tile), lambda t: (0, t))
    down = pl.BlockSpec((tile, n), lambda t: (t, 0))
    sums = [across] * 4 + [down] * 2
    out_specs = list(sums)
    out_shape = [jax.ShapeDtypeStruct((n, hidden), f32)] * 4 + [jax.ShapeDtypeStruct((hidden, n), f32)] * 2
    if own:
        out_specs += [pl.BlockSpec((count, tile), lambda t: (0, t))] * 3
        out_shape += [jax.ShapeDtypeStruct((count, hidden), bf16)] * 3
    columns = pl.BlockSpec((width, tile), lambda t: (0, t))
    in_specs = [whole(nm.shape), whole(go.shape), whole(nm_columns.shape), whole(go_columns.shape)]
    in_specs += [columns, columns, pl.BlockSpec((tile, width), lambda t: (t, 0))]
    in_specs += sums if previous else []
    return pl.pallas_call(
        functools.partial(ffn_kernel, own, bool(previous)),
        grid=(pl.cdiv(hidden, tile),),
        in_specs=in_specs,
        out_specs=out_specs,
        out_shape=out_shape,
        compiler_params=pltpu.CompilerParams(vmem_limit_bytes=56 * 2**20),
        cost_estimate=light,
    )(nm, go, nm_columns, go_columns, w_gate, w_up, w_down, *previous)


def shards(
    sizes,
    inputs,
    seq_lengths,
    norm_in,
    w_query,
    w_key,
    w_value,
    w_out,
    norm_mid,
    w_gate,
    w_up,
    w_down,
    out_cotangent,
    kv_cotangent,
):
    n_outer, n_dp = sizes
    seq_len, width = inputs.shape
    half, quarter = seq_len // 2, seq_len // 4
    head = w_key.shape[1]
    own_heads = w_query.shape[1]
    scale = head ** (-0.5)
    rows = width // n_dp
    z, x = lax.axis_index("z"), lax.axis_index("x")
    order = Order()
    run, swap, wait = order.run, order.swap, order.wait
    one = jnp.minimum(seq_lengths[0], 1).astype(f32)
    me = 2 * lax.axis_index("c") + lax.axis_index("y")
    quarters = jnp.stack([me ^ k for k in range(4)]).astype(jnp.int32)
    others = [lax.rem(z + k, GROUP) for k in range(1, GROUP)]
    places = jnp.stack([2 * z + 1 - x, 2 * z + x, *others]).astype(jnp.int32)
    positions = (quarters[:, None] * quarter + jnp.arange(quarter, dtype=jnp.int32)[None, :]).reshape(seq_len)
    gain_in, gain_mid = norm_in.reshape(1, width), norm_mid.reshape(1, width)
    ones = jnp.ones_like(norm_mid)
    same, crossed = rotary_tables(positions, head)
    masks = (same, crossed, positions[:, None], positions[None, :], seq_lengths.reshape(1, 1))
    weights = (w_gate, w_up, w_down)

    def shape(n, kind, count=seq_len):
        return jax.ShapeDtypeStruct((count, n), kind)

    def scaled(block):
        return block * inverse_rms(block)

    def remote(gathered):
        return [lax.dynamic_index_in_dim(gathered, k, 0, keepdims=False) for k in others]

    def columns(part):
        part = part.reshape(part.shape[0], n_outer, GROUP, 2, rows) if n_outer > 1 else part
        taken = []
        for which in (1 - x, x):
            if n_outer > 1:
                cut = lax.dynamic_index_in_dim(part, z, 2, keepdims=False)
                cut = lax.dynamic_index_in_dim(cut, which, 2, keepdims=False)
                taken.append(cut.reshape(part.shape[0], n_outer * rows))
            else:
                taken.append(lax.dynamic_slice_in_dim(part, (2 * z + which) * rows, rows, 1))
        return jnp.concatenate(taken, axis=1)

    def packed(blocks, gain):
        if n_outer == 1:
            return run(lambda *blocks: pack(blocks, gain, places, rows), *blocks)
        blocks = [b for a in blocks for b in (remote(a) if a.shape[0] == GROUP else list(a))]
        whole = run(lambda *blocks: (jnp.concatenate(blocks, axis=0) * (gain * one)).astype(bf16), *blocks)
        return whole, columns(whole)

    def add_y(kept, received):
        return kept[:quarter] + received

    def wgrads(*args):
        return ffn(*args[:4], *weights, previous=args[4:])

    inputs, grad_down_in, kv_cotangent, go_quarter = run(
        arrange, quarters, seq_lengths, inputs, out_cotangent, kv_cotangent
    )
    go_z = lax.all_gather(go_quarter, "z", axis=0, tiled=False)

    kept, sent, normed, queries, key_rot, value_rows, attended = run(
        lambda *args: call(
            functools.partial(forward_kernel, scale),
            "attention_forward",
            args,
            [shape(width, f32, half), shape(width, f32, half), shape(width, bf16), shape(own_heads, bf16),
             shape(head, bf16), shape(head, bf16), shape(own_heads, bf16)],
        ),
        inputs, gain_in, w_query, w_key, w_value, w_out, *masks,
    )
    sent = swap(sent, "c")
    go_own_columns = run(columns, grad_down_in)
    kept = run(jnp.add, kept, sent)
    received = swap(kept[quarter:], "y")

    def hidden_of(kept, received, inputs):
        own = add_y(kept, received) + inputs.astype(f32)
        return own, scaled(own)

    own, scaled_own = run(hidden_of, kept, received, inputs[:quarter])
    nm_z_own = lax.all_gather(scaled_own, "z", axis=0, tiled=False)
    other = swap(own, "y")
    far_own = swap(own, "c")
    scaled_other = run(scaled, other)
    nm_z_other = lax.all_gather(scaled_other, "z", axis=0, tiled=False)
    far_other = swap(other, "c")
    hidden = [own, other, far_own, far_other]

    picked = [(2 * rows, bf16)] if n_outer == 1 else []
    normed_mid, *nm_own_columns = run(
        lambda *hidden: rows_call(
            mid_kernel, "mid_norm", [hidden], [], [gain_mid], [(width, bf16), *picked], 0, prefetch=(places,)
        ),
        *hidden,
    )
    normed_mid = normed_mid.reshape(seq_len, width)
    nm_own_columns = nm_own_columns[0].reshape(seq_len, 2 * rows) if n_outer == 1 else columns(normed_mid)
    go_z = wait(go_z)
    go_first = run(lambda a: lax.dynamic_index_in_dim(a, others[0], 0), go_z)
    go_first = swap(go_first, "y")
    go_far = swap(go_z, "c")
    *sums, mixed, grad_gate, grad_up = run(
        lambda *args: ffn(*args, *weights, own=True),
        normed_mid, grad_down_in, nm_own_columns, go_own_columns,
    )
    go_first = wait(go_first)
    mid_kept, mid_sent = run(
        lambda *args: pair_dots("mid_part", args[:2], args[2:], True), grad_gate, grad_up, w_gate, w_up
    )
    mid_sent = swap(mid_sent, "c")
    kept = run(jnp.add, mid_kept, mid_sent)
    received = swap(kept[quarter:], "y")
    go_rest = run(lambda a: jnp.concatenate([lax.dynamic_index_in_dim(a, k, 0) for k in others[1:]], axis=0), go_z)
    go, go_columns = packed([go_z, go_far], ones)
    own = run(add_y, kept, received)
    other = swap(own, "y")
    far_own = swap(own, "c")
    down_kept, down_sent = run(lambda *args: pair_dots("down_part", args[:1], args[1:], False), mixed, w_down)
    nm_z_own = wait(nm_z_own)
    nm_far = swap(nm_z_own, "c")
    down_sent = swap(down_sent, "c")
    other = wait(other)
    go_rest = order.move(go_rest, "y", [(0, 1), (1, 0)], queue=False)
    grad_mid = [own, other, far_own, swap(other, "c")]
    grad_hidden, grad_attention, grad_norm_mid = run(
        lambda *args: rows_call(
            mid_back_kernel, "mid_back", [args[:4], args[4:]], [grad_down_in.reshape(4, quarter, width)], [gain_mid],
            [(width, f32), (width, bf16)], 1,
        ),
        *grad_mid, *hidden,
    )
    grad_attention = grad_attention.reshape(seq_len, width)

    if n_outer == 1:
        at_x = 2 * jnp.arange(GROUP, dtype=jnp.int32)
        at_x = jnp.concatenate([at_x + 1 - x, at_x + x])
        (out_sent,) = run(
            lambda *args: placed_call(out_kernel, "out_grad", at_x, args, [shape(width // 2, f32, own_heads)]),
            attended, grad_attention,
        )
    else:
        out_sent = run(dot_tn, attended, by_x(grad_attention, 1 - x, rows))
    out_sent = swap(out_sent, "x")
    nm, nm_columns = packed([nm_z_own, nm_far], norm_mid)
    down_kept = run(jnp.add, down_kept, down_sent)
    kept, sent, kv_kept, kv_sent, grad_query = run(
        lambda *args: call(
            functools.partial(backward_kernel, scale),
            "attention_backward",
            args,
            [shape(width, f32, half), shape(width, f32, half), shape(2 * head, f32, half), shape(2 * head, f32, half),
             shape(own_heads, bf16)],
        ),
        grad_attention, w_out, w_query, queries, key_rot, value_rows, *masks,
    )
    sent = swap(sent, "c")
    kv_sent = swap(kv_sent, "c")
    if n_outer == 1:
        out_kept, query_sent, query_kept = run(
            lambda *args: placed_call(
                late_kernel, "late_grads", at_x, args,
                [shape(width // 2, f32, own_heads), shape(own_heads, f32, width // 2), shape(own_heads, f32, width // 2)],
            ),
            attended, grad_attention, normed, grad_query,
        )
    else:
        out_kept = run(dot_tn, attended, by_x(grad_attention, x, rows))
        query_sent = run(dot_tn, by_x(normed, 1 - x, rows), grad_query)
        query_kept = run(dot_tn, by_x(normed, x, rows), grad_query)

    query_sent = order.move(query_sent, "x", [(0, 1), (1, 0)], queue=False)

    sums = run(wgrads, nm, go, nm_columns, go_columns, *sums)
    go_rest = wait(go_rest)
    out_half = run(jnp.add, out_kept, out_sent)
    kv_kept = run(jnp.add, kv_kept, kv_sent)
    kv_received = order.move(kv_kept[quarter:], "y", [(0, 1), (1, 0)], queue=False)
    kept = run(jnp.add, kept, sent)
    received = swap(kept[quarter:], "y")
    down_received = order.move(down_kept[quarter:], "y", [(0, 1), (1, 0)], queue=False)
    nm_z_other = wait(nm_z_other)
    nm_far = swap(nm_z_other, "c")
    go_far = [swap(go_first, "c"), swap(go_rest, "c")]
    grad_w_out = lax.psum_scatter(out_half, ("o", "z"), scatter_dimension=1, tiled=True)
    go, go_columns = packed([go_first, go_rest, *go_far], ones)
    nm, nm_columns = packed([nm_z_other, nm_far], norm_mid)
    sums = run(wgrads, nm, go, nm_columns, go_columns, *sums)
    gate_sent = swap(sums[0], "x")
    summed_own = run(add_y, kept, received)
    summed_other = order.move(summed_own, "y", [(0, 1), (1, 0)], queue=False)
    kv_own = run(add_y, kv_kept, kv_received)
    kv_other = order.move(kv_own, "y", [(0, 1), (1, 0)], queue=False)
    down_own = run(add_y, down_kept, down_received)
    down_other = order.move(down_own, "y", [(0, 1), (1, 0)], queue=False)
    query_half = run(jnp.add, query_kept, query_sent)
    grad_w_query = lax.psum_scatter(query_half, ("o", "z"), scatter_dimension=0, tiled=True)
    up_sent = order.move(sums[2], "x", [(0, 1), (1, 0)], queue=False)
    grad_w_gate = run(jnp.add, sums[1], gate_sent)
    summed_other = wait(summed_other)

    far = [swap(a, "c") for a in (kv_own, kv_other, summed_own, summed_other)]

    def key_value(*parts):
        grad_kv = jnp.concatenate(parts, axis=0) + kv_cotangent
        grad_key = grad_kv[:, :head]
        crossed_key = jnp.concatenate([grad_key[:, head // 2 :], grad_key[:, : head // 2]], axis=1)
        return (grad_key * same - crossed_key * crossed).astype(bf16), grad_kv[:, head:].astype(bf16)

    grad_key, grad_value = run(key_value, kv_own, kv_other, far[0], far[1])
    keyed = run(lambda k, v: dot_nt(k, w_key) + dot_nt(v, w_value), grad_key, grad_value)
    grad_inputs, grad_norm_in = run(
        lambda keyed, *summed: rows_call(
            in_back_kernel, "in_back", [summed],
            [keyed.reshape(4, quarter, width), inputs.reshape(4, quarter, width), grad_hidden], [gain_in],
            [(width, bf16)], 1, prefetch=(quarters,),
        ),
        keyed, summed_own, summed_other, far[2], far[3],
    )

    piece = rows // 4
    m = 2 * lax.axis_index("y") + lax.axis_index("c")

    def small_sums(grad_key, grad_value, grad_norm_in, grad_norm_mid):
        kv = jnp.concatenate([dot_tn(normed, grad_key), dot_tn(normed, grad_value)], axis=1)
        kv = lax.dynamic_index_in_dim(kv.reshape(n_dp, 4, piece, 2 * head), m, 1, keepdims=False)
        gains = jnp.concatenate([grad_norm_in, grad_norm_mid]).reshape(2, n_dp, rows).transpose(1, 0, 2)
        gains = jnp.pad(gains, ((0, 0), (0, 6), (0, 2 * head - rows)))
        small = jnp.concatenate([kv, gains], axis=1).reshape(n_dp // 2, 2, -1, 2 * head)
        return split(small, 1, x)

    small, small_sent = run(small_sums, grad_key, grad_value, grad_norm_in, grad_norm_mid)
    small_sent = order.move(small_sent, "x", [(0, 1), (1, 0)], queue=False)
    down_other = wait(down_other)
    small = run(jnp.add, small, small_sent).reshape(n_dp // 2, -1, 2 * head)
    last_sent = order.move(sums[4], "x", [(0, 1), (1, 0)], queue=False)
    grad_w_up = run(jnp.add, sums[3], up_sent)
    down = [down_own, down_other, swap(down_own, "c"), swap(down_other, "c")]
    (result,) = run(
        lambda *args: rows_call(
            add_kernel, "result", [args[:4], args[4:]], [], [], [(width, bf16)], 0, prefetch=(quarters,)
        ),
        *down, *hidden,
    )
    if n_outer == 1:
        small, small_sent = run(lambda a: split(a, 0, z // 2), small)
        small_sent = order.move(small_sent, "z", [(i, i ^ 2) for i in range(GROUP)], queue=False)
        small = run(jnp.add, small, small_sent)
        small, small_sent = run(lambda a: split(a, 0, z % 2), small)
        small_sent = order.move(small_sent, "z", [(i, i ^ 1) for i in range(GROUP)], queue=False)
        small = run(jnp.add, small, small_sent)
    else:
        small = lax.psum_scatter(small, ("o", "z"), scatter_dimension=0, tiled=True)
    kv = run(lambda a: lax.all_gather(a[0, :piece], ("y", "c"), axis=0, tiled=True), small)
    out_norm_in, out_norm_mid = small[0, piece, :rows], small[0, piece + 1, :rows]
    grad_w_down = run(jnp.add, sums[5], last_sent)
    if n_outer > 1:
        grad_w_down = lax.psum_scatter(grad_w_down, "o", scatter_dimension=1, tiled=True)
        grad_w_gate = lax.psum_scatter(grad_w_gate, "o", scatter_dimension=0, tiled=True)
        grad_w_up = lax.psum_scatter(grad_w_up, "o", scatter_dimension=0, tiled=True)

    return (
        result.reshape(seq_len, width),
        grad_inputs.reshape(seq_len, width),
        out_norm_in,
        grad_w_query,
        kv[:, :head],
        kv[:, head:],
        grad_w_out,
        out_norm_mid,
        grad_w_gate,
        grad_w_up,
        grad_w_down,
    )


def solution(mesh):
    n_dp = mesh.shape["dp"]
    n_outer = n_dp // (2 * GROUP)
    split = Mesh(mesh.devices.reshape(n_outer, GROUP, 2, 2, 2), ("o", "z", "x", "y", "c"))
    dp, mp = ("o", "z", "x"), ("y", "c")

    def program(*args):
        return shards((n_outer, n_dp), *args)

    return jax.shard_map(
        program,
        mesh=split,
        in_specs=(
            P(dp, None),
            P(dp),
            P(),
            P(None, mp),
            P(),
            P(),
            P(mp, None),
            P(),
            P(None, mp),
            P(None, mp),
            P(mp, None),
            P(dp, None),
            P(dp, None),
        ),
        out_specs=(
            P(dp, None),
            P(dp, None),
            P(dp),
            P(dp, mp),
            P(dp, None),
            P(dp, None),
            P(mp, dp),
            P(dp),
            P(dp, mp),
            P(dp, mp),
            P(mp, dp),
        ),
        check_vma=False,
    )
```

```python
import functools

import jax
import jax.numpy as jnp
from jax import lax
from jax.experimental import pallas as pl
from jax.experimental.pallas import tpu as pltpu
from jax.sharding import Mesh, PartitionSpec as P

epsilon = 1e-06
masked_value = -1e30
GROUP = 4
f32 = jnp.float32
bf16 = jnp.bfloat16

light = pl.CostEstimate(flops=1, bytes_accessed=1, transcendentals=0)


def dot(a, b):
    return jnp.dot(a, b, preferred_element_type=f32)


def dot_nt(a, b):
    return lax.dot_general(a, b, (((1,), (1,)), ((), ())), preferred_element_type=f32)


def dot_tn(a, b):
    return lax.dot_general(a, b, (((0,), (0,)), ((), ())), preferred_element_type=f32)


def arrange_kernel(places, length_ref, inputs_ref, cotangent_ref, kv_ref, inputs_out, cotangent_out, kv_out, quarter_out):
    k = pl.program_id(0)
    count = inputs_ref.shape[0]
    row = lax.broadcasted_iota(jnp.int32, (count, 1), 0) + places[k] * count
    valid = row < length_ref[0, 0]
    inputs_out[...] = inputs_ref[...]
    cotangent = jnp.where(valid, cotangent_ref[...].astype(f32), 0.0)
    cotangent_out[...] = cotangent.astype(bf16)
    kv_out[...] = jnp.where(valid, kv_ref[...].astype(f32), 0.0)

    @pl.when(k == 0)
    def _():
        quarter_out[...] = cotangent


def arrange(places, lengths, inputs, cotangent, kv):
    seq_len, width = inputs.shape
    q = seq_len // 4
    kv_width = kv.shape[1]
    picked = pl.BlockSpec((q, width), lambda k, p: (p[k], 0))
    placed = pl.BlockSpec((q, width), lambda k, p: (k, 0))
    return pl.pallas_call(
        arrange_kernel,
        grid_spec=pltpu.PrefetchScalarGridSpec(
            num_scalar_prefetch=1,
            grid=(4,),
            in_specs=[
                pl.BlockSpec((1, 1), lambda k, p: (0, 0)),
                picked,
                picked,
                pl.BlockSpec((q, kv_width), lambda k, p: (p[k], 0)),
            ],
            out_specs=[
                placed,
                placed,
                pl.BlockSpec((q, kv_width), lambda k, p: (k, 0)),
                pl.BlockSpec((q, width), lambda k, p: (0, 0)),
            ],
        ),
        out_shape=[
            jax.ShapeDtypeStruct((seq_len, width), bf16),
            jax.ShapeDtypeStruct((seq_len, width), bf16),
            jax.ShapeDtypeStruct((seq_len, kv_width), f32),
            jax.ShapeDtypeStruct((q, width), f32),
        ],
        name="arrange",
        compiler_params=pltpu.CompilerParams(vmem_limit_bytes=32 * 2**20),
        cost_estimate=light,
    )(places, lengths.reshape(1, 1), inputs, cotangent, kv)


def rotary_tables(positions, size):
    half_size = size // 2
    inverse = 10000.0 ** (-2.0 * jnp.arange(half_size, dtype=f32) / size)
    angles = positions.astype(f32)[:, None] * inverse[None, :]
    cosine, sine = jnp.cos(angles), jnp.sin(angles)
    return jnp.concatenate([cosine, cosine], axis=1), jnp.concatenate([-sine, sine], axis=1)


def rotate(values, same, crossed):
    return values * same + pltpu.roll(values, values.shape[-1] // 2, 1) * crossed


def norm_back(stream, inverse_rms, gain, grad_normed):
    weighted = gain * grad_normed
    return inverse_rms * weighted - stream * inverse_rms**3 * jnp.mean(weighted * stream, axis=-1, keepdims=True)


def inverse_rms(block):
    return lax.rsqrt(jnp.mean(block * block, axis=-1, keepdims=True) + epsilon)


def pack_kernel(n, places, *refs):
    blocks, (scale, out, picked) = refs[:n], refs[n:]
    width = picked.shape[2] // 2
    for j in range(n):
        out[j] = (blocks[j][0] * scale[...]).astype(bf16)
        for part in range(2):
            at = pl.ds(pl.multiple_of(places[part] * width, width), width)
            picked[j, :, part * width : (part + 1) * width] = (blocks[j][0, :, at] * scale[:, at]).astype(bf16)


def pack(blocks, scale, places, rows, tile=32):
    count, width = blocks[0].shape[1:]
    args, specs = [], []
    for a in blocks:
        for k in range(GROUP - 1 if a.shape[0] == GROUP else a.shape[0]):
            args.append(a)
            if a.shape[0] == GROUP:
                specs.append(pl.BlockSpec((1, tile, width), lambda t, p, k=k: (p[2 + k], t, 0)))
            else:
                specs.append(pl.BlockSpec((1, tile, width), lambda t, p, k=k: (k, t, 0)))
    n = len(args)
    out, picked = pl.pallas_call(
        functools.partial(pack_kernel, n),
        grid_spec=pltpu.PrefetchScalarGridSpec(
            num_scalar_prefetch=1,
            grid=(count // tile,),
            in_specs=specs + [pl.BlockSpec((1, width), lambda t, p: (0, 0))],
            out_specs=[
                pl.BlockSpec((n, tile, width), lambda t, p: (0, t, 0)),
                pl.BlockSpec((n, tile, 2 * rows), lambda t, p: (0, t, 0)),
            ],
        ),
        out_shape=[
            jax.ShapeDtypeStruct((n, count, width), bf16),
            jax.ShapeDtypeStruct((n, count, 2 * rows), bf16),
        ],
        name="pack",
        compiler_params=pltpu.CompilerParams(vmem_limit_bytes=32 * 2**20),
        cost_estimate=light,
    )(places, *args, scale.reshape(1, width))
    return out.reshape(n * count, width), picked.reshape(n * count, 2 * rows)


class Order:
    def __init__(self):
        self.core = ()
        self.links = {}

    def run(self, f, *args):
        n = len(args)
        args = lax.optimization_barrier((*args, *self.core))[:n]
        outs = f(*args)
        self.core = tuple(outs)[:1] if isinstance(outs, (list, tuple)) else (outs,)
        return outs

    def wait(self, a):
        (a,) = self.run(lambda a: lax.optimization_barrier((a,)), a)
        return a

    def move(self, a, axis, pairs, queue=True):
        before = self.links.get(axis, ()) if queue else ()
        a = lax.optimization_barrier((a, *self.core, *before))[0]
        a = lax.ppermute(a, axis, pairs)
        if queue:
            self.links[axis] = (a,)
        return a

    def swap(self, a, axis):
        return self.move(a, axis, [(0, 1), (1, 0)], queue=axis != "c")

    def pair_z(self, a, bit):
        return self.move(a, "z", [(i, i ^ bit) for i in range(GROUP)])


def split(a, axis, mine):
    n = a.shape[axis] // 2
    return lax.dynamic_slice_in_dim(a, mine * n, n, axis), lax.dynamic_slice_in_dim(a, (1 - mine) * n, n, axis)


def by_x(a, which, rows):
    n = a.shape[1] // (2 * rows)
    return jnp.concatenate([lax.dynamic_slice_in_dim(a, (2 * i + which) * rows, rows, 1) for i in range(n)], axis=1)


def call(kernel, name, ins, outs):
    return pl.pallas_call(
        kernel,
        out_shape=outs,
        name=name,
        compiler_params=pltpu.CompilerParams(vmem_limit_bytes=56 * 2**20),
        cost_estimate=light,
    )(*ins)


def probabilities(q, k, allowed, scale):
    scores = jnp.where(allowed, dot_nt(q, k) * scale, masked_value)
    exponent = jnp.exp(scores - jnp.max(scores, axis=-1, keepdims=True))
    return exponent / jnp.sum(exponent, axis=-1, keepdims=True)


def forward_kernel(
    scale, x_ref, gain_ref, wq_ref, wk_ref, wv_ref, wo_ref, same_ref, crossed_ref, pos_q_ref, pos_k_ref, length_ref,
    kept_ref, sent_ref, normed_ref, q_ref, k_ref, v_ref, attended_ref,
):
    stream = x_ref[...].astype(f32)
    normed_ref[...] = (stream * inverse_rms(stream) * gain_ref[...]).astype(bf16)
    normed = normed_ref[...]
    same, crossed = same_ref[...], crossed_ref[...]
    k = rotate(dot(normed, wk_ref[...]), same, crossed).astype(bf16)
    v = dot(normed, wv_ref[...]).astype(bf16)
    k_ref[...], v_ref[...] = k, v
    raw = dot(normed, wq_ref[...])
    length = length_ref[0, 0]
    allowed = (pos_k_ref[...] <= pos_q_ref[...]) & (pos_k_ref[...] < length)
    valid = (pos_q_ref[...] < length).astype(f32)
    size = k.shape[1]
    for h in range(raw.shape[1] // size):
        at = slice(h * size, (h + 1) * size)
        q = rotate(raw[:, at], same, crossed).astype(bf16)
        q_ref[:, at] = q
        weights = probabilities(q, k, allowed, scale).astype(bf16)
        attended_ref[:, at] = (dot(weights, v) * valid).astype(bf16)
    n = kept_ref.shape[0]
    sent_ref[...] = dot(attended_ref[n:], wo_ref[...])
    kept_ref[...] = dot(attended_ref[:n], wo_ref[...])


def backward_kernel(
    scale, ga_ref, wo_ref, wq_ref, q_ref, k_ref, v_ref, same_ref, crossed_ref, pos_q_ref, pos_k_ref, length_ref,
    kept_ref, sent_ref, kv_kept_ref, kv_sent_ref, gq_ref,
):
    k, v = k_ref[...], v_ref[...]
    same, crossed = same_ref[...], crossed_ref[...]
    length = length_ref[0, 0]
    allowed = (pos_k_ref[...] <= pos_q_ref[...]) & (pos_k_ref[...] < length)
    valid = (pos_q_ref[...] < length).astype(f32)
    grad_attended = (dot_nt(ga_ref[...], wo_ref[...]) * valid).astype(bf16)
    size = k.shape[1]
    grad_key = grad_value = 0.0
    for h in range(grad_attended.shape[1] // size):
        at = slice(h * size, (h + 1) * size)
        q, g = q_ref[:, at], grad_attended[:, at]
        probs = probabilities(q, k, allowed, scale)
        grad_probs = dot_nt(g, v)
        delta = jnp.sum(probs * grad_probs, axis=-1, keepdims=True)
        grad_scores = (probs * (grad_probs - delta)).astype(bf16)
        gq_ref[:, at] = rotate(dot(grad_scores, k) * scale, same, -crossed).astype(bf16)
        grad_key += dot_tn(grad_scores, q)
        grad_value += dot_tn(probs.astype(bf16), g)
    n = kept_ref.shape[0]
    for ref, at in ((kv_kept_ref, slice(0, n)), (kv_sent_ref, slice(n, 2 * n))):
        ref[:, :size] = grad_key[at] * scale
        ref[:, size:] = grad_value[at]
    sent_ref[...] = dot_nt(gq_ref[n:], wq_ref[...])
    kept_ref[...] = dot_nt(gq_ref[:n], wq_ref[...])


def pair_kernel(transposed, *refs):
    n = (len(refs) - 2) // 2
    kept, sent = refs[2 * n :]
    half = kept.shape[0]
    for out, at in ((sent, slice(half, 2 * half)), (kept, slice(0, half))):
        total = 0.0
        for rows, matrix in zip(refs[:n], refs[n : 2 * n]):
            total += (dot_nt if transposed else dot)(rows[at, :], matrix[...])
        out[...] = total


def pair_dots(name, rows, matrices, transposed, tile=512):
    count, depth = rows[0].shape
    width = matrices[0].shape[0 if transposed else 1]
    whole = pl.BlockSpec((count, depth), lambda t: (0, 0), pipeline_mode=pl.Buffered(1))
    part = pl.BlockSpec((tile, depth), lambda t: (t, 0)) if transposed else pl.BlockSpec((depth, tile), lambda t: (0, t))
    return pl.pallas_call(
        functools.partial(pair_kernel, transposed),
        grid=(width // tile,),
        in_specs=[whole] * len(rows) + [part] * len(matrices),
        out_specs=[pl.BlockSpec((count // 2, tile), lambda t: (0, t))] * 2,
        out_shape=[jax.ShapeDtypeStruct((count // 2, width), f32)] * 2,
        name=name,
        compiler_params=pltpu.CompilerParams(vmem_limit_bytes=48 * 2**20),
        cost_estimate=light,
    )(*rows, *matrices)


def out_kernel(places, left_ref, right_ref, out_ref):
    width = out_ref.shape[1] // GROUP
    for i in range(GROUP):
        at = pl.ds(pl.multiple_of(places[i] * width, width), width)
        out_ref[:, i * width : (i + 1) * width] = dot_tn(left_ref[...], right_ref[:, at])


def late_kernel(places, attended_ref, ga_ref, normed_ref, gq_ref, out_ref, sent_ref, kept_ref):
    width = out_ref.shape[1] // GROUP
    for i in range(GROUP):
        rows = slice(i * width, (i + 1) * width)
        sent = pl.ds(pl.multiple_of(places[i] * width, width), width)
        kept = pl.ds(pl.multiple_of(places[GROUP + i] * width, width), width)
        sent_ref[rows] = dot_tn(normed_ref[:, sent], gq_ref[...])
        kept_ref[rows] = dot_tn(normed_ref[:, kept], gq_ref[...])
        out_ref[:, rows] = dot_tn(attended_ref[...], ga_ref[:, kept])


def placed_call(kernel, name, places, ins, outs):
    def whole(shape):
        return pl.BlockSpec(shape, lambda t, p: (0,) * len(shape), pipeline_mode=pl.Buffered(1))

    return pl.pallas_call(
        kernel,
        grid_spec=pltpu.PrefetchScalarGridSpec(
            num_scalar_prefetch=1,
            grid=(1,),
            in_specs=[whole(a.shape) for a in ins],
            out_specs=[pl.BlockSpec(a.shape, lambda t, p: (0,) * len(a.shape)) for a in outs],
        ),
        out_shape=outs,
        name=name,
        compiler_params=pltpu.CompilerParams(vmem_limit_bytes=48 * 2**20),
        cost_estimate=light,
    )(places, *ins)


def rows_call(kernel, name, quarters, stacked, shared, outs, totals, tile=16, prefetch=()):
    count, width = quarters[0][0].shape
    args = [a for group in quarters for a in group] + list(stacked) + list(shared)
    specs = [pl.BlockSpec((tile, width), lambda t, *p: (t, 0))] * (4 * len(quarters))
    specs += [pl.BlockSpec((4, tile, a.shape[2]), lambda t, *p: (0, t, 0)) for a in stacked]
    specs += [pl.BlockSpec(a.shape, lambda t, *p: (0, 0)) for a in shared]
    out_specs = [pl.BlockSpec((4, tile, w), lambda t, *p: (0, t, 0)) for w, _ in outs]
    out_specs += [pl.BlockSpec((1, width), lambda t, *p: (0, 0))] * totals
    out_shape = [jax.ShapeDtypeStruct((4, count, w), kind) for w, kind in outs]
    out_shape += [jax.ShapeDtypeStruct((1, width), f32)] * totals
    return pl.pallas_call(
        kernel,
        grid_spec=pltpu.PrefetchScalarGridSpec(
            num_scalar_prefetch=len(prefetch), grid=(count // tile,), in_specs=specs, out_specs=out_specs
        ),
        out_shape=out_shape,
        name=name,
        compiler_params=pltpu.CompilerParams(vmem_limit_bytes=32 * 2**20),
        cost_estimate=light,
    )(*prefetch, *args)


def mid_kernel(places, *refs):
    hidden, (gain, out), picked = refs[:4], refs[4:6], refs[6:]
    for j in range(4):
        h = hidden[j][...]
        r = inverse_rms(h)
        out[j] = (h * r * gain[...]).astype(bf16)
        for part in range(2 * len(picked)):
            n = picked[0].shape[2] // 2
            at = pl.ds(pl.multiple_of(places[part] * n, n), n)
            picked[0][j, :, part * n : (part + 1) * n] = (hidden[j][:, at] * r * gain[:, at]).astype(bf16)


def mid_back_kernel(*refs):
    grads, hidden, (grad_out, gain, grad_hidden, rounded, total) = refs[:4], refs[4:8], refs[8:]
    gain = gain[...]
    acc = 0.0
    for j in range(4):
        h, g = hidden[j][...], grads[j][...]
        r = inverse_rms(h)
        acc += jnp.sum(g * h * r, axis=0, keepdims=True)
        back = grad_out[j].astype(f32) + norm_back(h, r, gain, g)
        grad_hidden[j] = back
        rounded[j] = back.astype(bf16)

    @pl.when(pl.program_id(0) == 0)
    def _():
        total[...] = jnp.zeros_like(total)

    total[...] += acc


def in_back_kernel(places, *refs):
    sums, (keyed, inputs, grad_hidden, gain, out, total) = refs[:4], refs[4:]
    gain = gain[...]
    acc = 0.0
    for j in range(4):
        stream = inputs[j].astype(f32)
        g = sums[j][...] + keyed[j]
        r = inverse_rms(stream)
        acc += jnp.sum(g * stream * r, axis=0, keepdims=True)
        out[places[j]] = (grad_hidden[j] + norm_back(stream, r, gain, g)).astype(bf16)

    @pl.when(pl.program_id(0) == 0)
    def _():
        total[...] = jnp.zeros_like(total)

    total[...] += acc


def add_kernel(places, *refs):
    left, right, (out,) = refs[:4], refs[4:8], refs[8:]
    for j in range(4):
        out[places[j]] = (left[j][...] + right[j][...]).astype(bf16)


def ffn_kernel(own, has_prev, *refs):
    nm_ref, go_ref, nmc_ref, goc_ref, wg_ref, wu_ref, wd_ref = refs[:7]
    previous = refs[7:13] if has_prev else None
    outs = refs[13:] if has_prev else refs[7:]
    gate = dot(nm_ref[...], wg_ref[...])
    up = dot(nm_ref[...], wu_ref[...])
    grad_mixed = dot_nt(go_ref[...], wd_ref[...]).astype(bf16).astype(f32)
    sig = jax.nn.sigmoid(gate)
    gate_sig = gate * sig
    mixed = (gate_sig * up).astype(bf16)
    grad_gate = (grad_mixed * up * sig * (1.0 + gate * (1.0 - sig))).astype(bf16)
    grad_up = (grad_mixed * gate_sig).astype(bf16)
    n = nmc_ref.shape[1] // 2
    by_gate = dot_tn(nmc_ref[...], grad_gate)
    by_up = dot_tn(nmc_ref[...], grad_up)
    by_down = dot_tn(mixed, goc_ref[...])
    sums = (by_gate[:n], by_gate[n:], by_up[:n], by_up[n:], by_down[:, :n], by_down[:, n:])
    for i in range(6):
        outs[i][...] = sums[i] + previous[i][...] if has_prev else sums[i]
    if own:
        outs[6][...] = mixed
        outs[7][...] = grad_gate
        outs[8][...] = grad_up


def ffn(nm, go, nm_columns, go_columns, w_gate, w_up, w_down, previous=(), own=False, tile=512):
    count, width = nm.shape
    hidden = w_gate.shape[1]
    n = nm_columns.shape[1] // 2

    def whole(shape):
        return pl.BlockSpec(shape, lambda t: (0, 0), pipeline_mode=pl.Buffered(1))

    across = pl.BlockSpec((n, tile), lambda t: (0, t))
    down = pl.BlockSpec((tile, n), lambda t: (t, 0))
    sums = [across] * 4 + [down] * 2
    out_specs = list(sums)
    out_shape = [jax.ShapeDtypeStruct((n, hidden), f32)] * 4 + [jax.ShapeDtypeStruct((hidden, n), f32)] * 2
    if own:
        out_specs += [pl.BlockSpec((count, tile), lambda t: (0, t))] * 3
        out_shape += [jax.ShapeDtypeStruct((count, hidden), bf16)] * 3
    columns = pl.BlockSpec((width, tile), lambda t: (0, t))
    in_specs = [whole(nm.shape), whole(go.shape), whole(nm_columns.shape), whole(go_columns.shape)]
    in_specs += [columns, columns, pl.BlockSpec((tile, width), lambda t: (t, 0))]
    in_specs += sums if previous else []
    return pl.pallas_call(
        functools.partial(ffn_kernel, own, bool(previous)),
        grid=(pl.cdiv(hidden, tile),),
        in_specs=in_specs,
        out_specs=out_specs,
        out_shape=out_shape,
        compiler_params=pltpu.CompilerParams(vmem_limit_bytes=56 * 2**20),
        cost_estimate=light,
    )(nm, go, nm_columns, go_columns, w_gate, w_up, w_down, *previous)


def shards(
    sizes,
    inputs,
    seq_lengths,
    norm_in,
    w_query,
    w_key,
    w_value,
    w_out,
    norm_mid,
    w_gate,
    w_up,
    w_down,
    out_cotangent,
    kv_cotangent,
):
    n_outer, n_dp = sizes
    seq_len, width = inputs.shape
    half, quarter = seq_len // 2, seq_len // 4
    head = w_key.shape[1]
    own_heads = w_query.shape[1]
    scale = head ** (-0.5)
    rows = width // n_dp
    z, x = lax.axis_index("z"), lax.axis_index("x")
    order = Order()
    run, swap, wait = order.run, order.swap, order.wait
    one = jnp.minimum(seq_lengths[0], 1).astype(f32)
    me = 2 * lax.axis_index("c") + lax.axis_index("y")
    quarters = jnp.stack([me ^ k for k in range(4)]).astype(jnp.int32)
    others = [lax.rem(z + k, GROUP) for k in range(1, GROUP)]
    places = jnp.stack([2 * z + 1 - x, 2 * z + x, *others]).astype(jnp.int32)
    positions = (quarters[:, None] * quarter + jnp.arange(quarter, dtype=jnp.int32)[None, :]).reshape(seq_len)
    gain_in, gain_mid = norm_in.reshape(1, width), norm_mid.reshape(1, width)
    ones = jnp.ones_like(norm_mid)
    same, crossed = rotary_tables(positions, head)
    masks = (same, crossed, positions[:, None], positions[None, :], seq_lengths.reshape(1, 1))
    weights = (w_gate, w_up, w_down)

    def shape(n, kind, count=seq_len):
        return jax.ShapeDtypeStruct((count, n), kind)

    def scaled(block):
        return block * inverse_rms(block)

    def remote(gathered):
        return [lax.dynamic_index_in_dim(gathered, k, 0, keepdims=False) for k in others]

    def columns(part):
        part = part.reshape(part.shape[0], n_outer, GROUP, 2, rows) if n_outer > 1 else part
        taken = []
        for which in (1 - x, x):
            if n_outer > 1:
                cut = lax.dynamic_index_in_dim(part, z, 2, keepdims=False)
                cut = lax.dynamic_index_in_dim(cut, which, 2, keepdims=False)
                taken.append(cut.reshape(part.shape[0], n_outer * rows))
            else:
                taken.append(lax.dynamic_slice_in_dim(part, (2 * z + which) * rows, rows, 1))
        return jnp.concatenate(taken, axis=1)

    def packed(blocks, gain):
        if n_outer == 1:
            return run(lambda *blocks: pack(blocks, gain, places, rows), *blocks)
        blocks = [b for a in blocks for b in (remote(a) if a.shape[0] == GROUP else list(a))]
        whole = run(lambda *blocks: (jnp.concatenate(blocks, axis=0) * (gain * one)).astype(bf16), *blocks)
        return whole, columns(whole)

    def add_y(kept, received):
        return kept[:quarter] + received

    def wgrads(*args):
        return ffn(*args[:4], *weights, previous=args[4:])

    inputs, grad_down_in, kv_cotangent, go_quarter = run(
        arrange, quarters, seq_lengths, inputs, out_cotangent, kv_cotangent
    )
    go_z = lax.all_gather(go_quarter, "z", axis=0, tiled=False)

    kept, sent, normed, queries, key_rot, value_rows, attended = run(
        lambda *args: call(
            functools.partial(forward_kernel, scale),
            "attention_forward",
            args,
            [shape(width, f32, half), shape(width, f32, half), shape(width, bf16), shape(own_heads, bf16),
             shape(head, bf16), shape(head, bf16), shape(own_heads, bf16)],
        ),
        inputs, gain_in, w_query, w_key, w_value, w_out, *masks,
    )
    sent = swap(sent, "c")
    go_own_columns = run(columns, grad_down_in)
    kept = run(jnp.add, kept, sent)
    received = swap(kept[quarter:], "y")

    def hidden_of(kept, received, inputs):
        own = add_y(kept, received) + inputs.astype(f32)
        return own, scaled(own)

    own, scaled_own = run(hidden_of, kept, received, inputs[:quarter])
    nm_z_own = lax.all_gather(scaled_own, "z", axis=0, tiled=False)
    other = swap(own, "y")
    far_own = swap(own, "c")
    scaled_other = run(scaled, other)
    nm_z_other = lax.all_gather(scaled_other, "z", axis=0, tiled=False)
    far_other = swap(other, "c")
    hidden = [own, other, far_own, far_other]

    picked = [(2 * rows, bf16)] if n_outer == 1 else []
    normed_mid, *nm_own_columns = run(
        lambda *hidden: rows_call(
            mid_kernel, "mid_norm", [hidden], [], [gain_mid], [(width, bf16), *picked], 0, prefetch=(places,)
        ),
        *hidden,
    )
    normed_mid = normed_mid.reshape(seq_len, width)
    nm_own_columns = nm_own_columns[0].reshape(seq_len, 2 * rows) if n_outer == 1 else columns(normed_mid)
    go_z = wait(go_z)
    go_first = run(lambda a: lax.dynamic_index_in_dim(a, others[0], 0), go_z)
    go_first = swap(go_first, "y")
    go_far = swap(go_z, "c")
    *sums, mixed, grad_gate, grad_up = run(
        lambda *args: ffn(*args, *weights, own=True),
        normed_mid, grad_down_in, nm_own_columns, go_own_columns,
    )
    go_first = wait(go_first)
    mid_kept, mid_sent = run(
        lambda *args: pair_dots("mid_part", args[:2], args[2:], True), grad_gate, grad_up, w_gate, w_up
    )
    mid_sent = swap(mid_sent, "c")
    kept = run(jnp.add, mid_kept, mid_sent)
    received = swap(kept[quarter:], "y")
    go_rest = run(lambda a: jnp.concatenate([lax.dynamic_index_in_dim(a, k, 0) for k in others[1:]], axis=0), go_z)
    go, go_columns = packed([go_z, go_far], ones)
    own = run(add_y, kept, received)
    other = swap(own, "y")
    far_own = swap(own, "c")
    down_kept, down_sent = run(lambda *args: pair_dots("down_part", args[:1], args[1:], False), mixed, w_down)
    nm_z_own = wait(nm_z_own)
    nm_far = swap(nm_z_own, "c")
    down_sent = swap(down_sent, "c")
    other = wait(other)
    go_rest = order.move(go_rest, "y", [(0, 1), (1, 0)], queue=False)
    grad_mid = [own, other, far_own, swap(other, "c")]
    grad_hidden, grad_attention, grad_norm_mid = run(
        lambda *args: rows_call(
            mid_back_kernel, "mid_back", [args[:4], args[4:]], [grad_down_in.reshape(4, quarter, width)], [gain_mid],
            [(width, f32), (width, bf16)], 1,
        ),
        *grad_mid, *hidden,
    )
    grad_attention = grad_attention.reshape(seq_len, width)

    if n_outer == 1:
        at_x = 2 * jnp.arange(GROUP, dtype=jnp.int32)
        at_x = jnp.concatenate([at_x + 1 - x, at_x + x])
        (out_sent,) = run(
            lambda *args: placed_call(out_kernel, "out_grad", at_x, args, [shape(width // 2, f32, own_heads)]),
            attended, grad_attention,
        )
    else:
        out_sent = run(dot_tn, attended, by_x(grad_attention, 1 - x, rows))
    out_sent = swap(out_sent, "x")
    nm, nm_columns = packed([nm_z_own, nm_far], norm_mid)
    down_kept = run(jnp.add, down_kept, down_sent)
    kept, sent, kv_kept, kv_sent, grad_query = run(
        lambda *args: call(
            functools.partial(backward_kernel, scale),
            "attention_backward",
            args,
            [shape(width, f32, half), shape(width, f32, half), shape(2 * head, f32, half), shape(2 * head, f32, half),
             shape(own_heads, bf16)],
        ),
        grad_attention, w_out, w_query, queries, key_rot, value_rows, *masks,
    )
    sent = swap(sent, "c")
    kv_sent = swap(kv_sent, "c")
    if n_outer == 1:
        out_kept, query_sent, query_kept = run(
            lambda *args: placed_call(
                late_kernel, "late_grads", at_x, args,
                [shape(width // 2, f32, own_heads), shape(own_heads, f32, width // 2), shape(own_heads, f32, width // 2)],
            ),
            attended, grad_attention, normed, grad_query,
        )
    else:
        out_kept = run(dot_tn, attended, by_x(grad_attention, x, rows))
        query_sent = run(dot_tn, by_x(normed, 1 - x, rows), grad_query)
        query_kept = run(dot_tn, by_x(normed, x, rows), grad_query)

    query_sent = order.move(query_sent, "x", [(0, 1), (1, 0)], queue=False)

    sums = run(wgrads, nm, go, nm_columns, go_columns, *sums)
    go_rest = wait(go_rest)
    out_sent, sent, kv_sent = wait(out_sent), wait(sent), wait(kv_sent)
    nm_z_other = wait(nm_z_other)
    nm_far = swap(nm_z_other, "c")
    go_far = [swap(go_first, "c"), swap(go_rest, "c")]
    out_half = run(jnp.add, out_kept, out_sent)
    grad_w_out = lax.psum_scatter(out_half, ("o", "z"), scatter_dimension=1, tiled=True)
    kv_kept = run(jnp.add, kv_kept, kv_sent)
    kv_received = order.move(kv_kept[quarter:], "y", [(0, 1), (1, 0)], queue=False)
    kept = run(jnp.add, kept, sent)
    received = swap(kept[quarter:], "y")
    down_received = order.move(down_kept[quarter:], "y", [(0, 1), (1, 0)], queue=False)
    go, go_columns = packed([go_first, go_rest, *go_far], ones)
    nm, nm_columns = packed([nm_z_other, nm_far], norm_mid)
    sums = run(wgrads, nm, go, nm_columns, go_columns, *sums)
    gate_sent = swap(sums[0], "x")
    summed_own = run(add_y, kept, received)
    summed_other = order.move(summed_own, "y", [(0, 1), (1, 0)], queue=False)
    kv_own = run(add_y, kv_kept, kv_received)
    kv_other = order.move(kv_own, "y", [(0, 1), (1, 0)], queue=False)
    down_own = run(add_y, down_kept, down_received)
    down_other = order.move(down_own, "y", [(0, 1), (1, 0)], queue=False)
    query_half = run(jnp.add, query_kept, query_sent)
    grad_w_query = lax.psum_scatter(query_half, ("o", "z"), scatter_dimension=0, tiled=True)
    up_sent = order.move(sums[2], "x", [(0, 1), (1, 0)], queue=False)
    grad_w_gate = run(jnp.add, sums[1], gate_sent)
    summed_other = wait(summed_other)

    far = [swap(a, "c") for a in (kv_own, kv_other, summed_own, summed_other)]

    def key_value(*parts):
        grad_kv = jnp.concatenate(parts, axis=0) + kv_cotangent
        grad_key = grad_kv[:, :head]
        crossed_key = jnp.concatenate([grad_key[:, head // 2 :], grad_key[:, : head // 2]], axis=1)
        return (grad_key * same - crossed_key * crossed).astype(bf16), grad_kv[:, head:].astype(bf16)

    grad_key, grad_value = run(key_value, kv_own, kv_other, far[0], far[1])
    keyed = run(lambda k, v: dot_nt(k, w_key) + dot_nt(v, w_value), grad_key, grad_value)
    grad_inputs, grad_norm_in = run(
        lambda keyed, *summed: rows_call(
            in_back_kernel, "in_back", [summed],
            [keyed.reshape(4, quarter, width), inputs.reshape(4, quarter, width), grad_hidden], [gain_in],
            [(width, bf16)], 1, prefetch=(quarters,),
        ),
        keyed, summed_own, summed_other, far[2], far[3],
    )

    piece = rows // 4
    m = 2 * lax.axis_index("y") + lax.axis_index("c")

    def small_sums(grad_key, grad_value, grad_norm_in, grad_norm_mid):
        kv = jnp.concatenate([dot_tn(normed, grad_key), dot_tn(normed, grad_value)], axis=1)
        kv = lax.dynamic_index_in_dim(kv.reshape(n_dp, 4, piece, 2 * head), m, 1, keepdims=False)
        gains = jnp.concatenate([grad_norm_in, grad_norm_mid]).reshape(2, n_dp, rows).transpose(1, 0, 2)
        gains = jnp.pad(gains, ((0, 0), (0, 6), (0, 2 * head - rows)))
        small = jnp.concatenate([kv, gains], axis=1).reshape(n_dp // 2, 2, -1, 2 * head)
        return split(small, 1, x)

    small, small_sent = run(small_sums, grad_key, grad_value, grad_norm_in, grad_norm_mid)
    small_sent = order.move(small_sent, "x", [(0, 1), (1, 0)], queue=False)
    down_other = wait(down_other)
    small = run(jnp.add, small, small_sent).reshape(n_dp // 2, -1, 2 * head)
    last_sent = order.move(sums[4], "x", [(0, 1), (1, 0)], queue=False)
    grad_w_up = run(jnp.add, sums[3], up_sent)
    down = [down_own, down_other, swap(down_own, "c"), swap(down_other, "c")]
    (result,) = run(
        lambda *args: rows_call(
            add_kernel, "result", [args[:4], args[4:]], [], [], [(width, bf16)], 0, prefetch=(quarters,)
        ),
        *down, *hidden,
    )
    if n_outer == 1:
        small, small_sent = run(lambda a: split(a, 0, z // 2), small)
        small_sent = order.move(small_sent, "z", [(i, i ^ 2) for i in range(GROUP)], queue=False)
        small = run(jnp.add, small, small_sent)
        small, small_sent = run(lambda a: split(a, 0, z % 2), small)
        small_sent = order.move(small_sent, "z", [(i, i ^ 1) for i in range(GROUP)], queue=False)
        small = run(jnp.add, small, small_sent)
    else:
        small = lax.psum_scatter(small, ("o", "z"), scatter_dimension=0, tiled=True)
    kv = run(lambda a: lax.all_gather(a[0, :piece], ("y", "c"), axis=0, tiled=True), small)
    out_norm_in, out_norm_mid = small[0, piece, :rows], small[0, piece + 1, :rows]
    grad_w_down = run(jnp.add, sums[5], last_sent)
    if n_outer > 1:
        grad_w_down = lax.psum_scatter(grad_w_down, "o", scatter_dimension=1, tiled=True)
        grad_w_gate = lax.psum_scatter(grad_w_gate, "o", scatter_dimension=0, tiled=True)
        grad_w_up = lax.psum_scatter(grad_w_up, "o", scatter_dimension=0, tiled=True)

    return (
        result.reshape(seq_len, width),
        grad_inputs.reshape(seq_len, width),
        out_norm_in,
        grad_w_query,
        kv[:, :head],
        kv[:, head:],
        grad_w_out,
        out_norm_mid,
        grad_w_gate,
        grad_w_up,
        grad_w_down,
    )


def solution(mesh):
    n_dp = mesh.shape["dp"]
    n_outer = n_dp // (2 * GROUP)
    split = Mesh(mesh.devices.reshape(n_outer, GROUP, 2, 2, 2), ("o", "z", "x", "y", "c"))
    dp, mp = ("o", "z", "x"), ("y", "c")

    def program(*args):
        return shards((n_outer, n_dp), *args)

    return jax.shard_map(
        program,
        mesh=split,
        in_specs=(
            P(dp, None),
            P(dp),
            P(),
            P(None, mp),
            P(),
            P(),
            P(mp, None),
            P(),
            P(None, mp),
            P(None, mp),
            P(mp, None),
            P(dp, None),
            P(dp, None),
        ),
        out_specs=(
            P(dp, None),
            P(dp, None),
            P(dp),
            P(dp, mp),
            P(dp, None),
            P(dp, None),
            P(mp, dp),
            P(dp),
            P(dp, mp),
            P(dp, mp),
            P(mp, dp),
        ),
        check_vma=False,
    )
```
